256 devices in a mesh: cell: 128 (over z, x, y), view: 2 (over core).
Axes of the slice: x: 4, y: 4, z: 8, core: 2. Of those that a mesh axis runs over, the one named last changes fastest.
Arguments:
- gauss_params: float32 [59, 4915200], P(None, ('cell', 'view')), as said below
- visible: int32 [4, 4915200], P(None, ('cell', 'view')), may hold values 0 or 1
- cameras: float32 [4, 15], replicated, as said below
- tile_ids: int32 [128, 2, 120], P('cell', 'view'), may hold values from 0 to 15359, as said below
- tile_blocks: int32 [128, 2, 120, 2], P('cell', 'view'), may hold values from -1 to 38399, as said below
- target: float32 [2, 3, 2048, 1920], P('view', None, 'cell'), as said below
Outputs:
- image: float32 [2, 3, 2048, 1920], P('view', None, 'cell')
- loss_map: float32 [2, 2048, 1920], P('view', 'cell')
The draws below stay inside these ranges and needn't reach their ends.
Inputs may be any that keep to these rules, and one draw needn't show every extreme that they name: `tile_ids`: for each view index v the lists of the 128 renderers (c, v) together name each of the 15360 tiles of views 2 v and 2 v + 1 exactly once. The tiles of one renderer lie in 120 different columns t % 120, at most 1 of them in one stripe t // 120, and some renderer reaches 1. `tile_blocks`: an entry names a block g (Gaussians 128 g to 128 g + 127, held by device g // 150 of cell+view) or is -1. The live entries of a tile come first, 1 to 2 of them, and some tile has 2. Every block is named by exactly one tile of all. The live entries of one renderer number exactly 150; at most 1 of them name blocks of one device, and every renderer reaches 1 with some device. `gauss_params`: rows 0 to 2: mean; 3 to 5: logarithms of the scales; 6 to 9: rotation quaternion, real part in row 6 between 1 and 2; row 10: opacity logit, at most 2; row 11 + 3 j + k: coefficient j of the spherical harmonics of colour channel k. Every Gaussian of a block named by a tile lies at depth about 4 to 40 in front of the camera of that tile's view. `cameras`: row w: a rotation (world to camera, row-major) in entries 0 to 8, the translation in 9 to 11, the focal length in pixels in 12 and the principal point (column, row) in 13 and 14. `target`: every value lies between 0.02 and 1.
All inputs are finite; a program needn't handle non-finite values. No bound on the sum of `visible` on one device may be relied on, other than what follows from the above.
Results may differ from the reference program's by a relative error of at most 0.0003.
Values sent between devices are 32-bit elements; how exact they have to be, the bound alone decides.
A program may use at most 64 MiB of HBM per device.

```python
import math
import jax
import jax.numpy as jnp
from jax import lax

GBLK = 128
FEAT = 59
IMG_W = 1920
BLK_DEV = 150
TILE_DEV = 120
LIST = 2
VIEWS = 4
IMG_H = 1024
ROWS = 2048
GAUSS = 4915200
CAP = 1
RCAP = 1
N_CELL = 128
N_VIEW = 2


def chain(left, right):
    return [[left[line][0] * right[0][column] + left[line][1] * right[1][column] + left[line][2] * right[2][column] for column in range(3)] for line in range(3)]


def camera_table(key):
    keys = jax.random.split(jax.random.fold_in(key, 101), 7)
    yaw = jax.random.uniform(keys[0], (VIEWS,), jnp.float32, -math.pi, math.pi)
    pitch = jax.random.uniform(keys[1], (VIEWS,), jnp.float32, -0.6, 0.6)
    roll = jax.random.uniform(keys[2], (VIEWS,), jnp.float32, -0.3, 0.3)
    offset = 30.0 * jax.random.normal(keys[3], (3, VIEWS), jnp.float32)
    focal_len = jax.random.uniform(keys[4], (VIEWS,), jnp.float32, 900.0, 1300.0)
    centre_col = 0.5 * IMG_W + jax.random.uniform(keys[5], (VIEWS,), jnp.float32, -30.0, 30.0)
    centre_row = 0.5 * IMG_H + jax.random.uniform(keys[6], (VIEWS,), jnp.float32, -30.0, 30.0)
    all_zero = jnp.zeros((VIEWS,), jnp.float32)
    all_one = jnp.ones((VIEWS,), jnp.float32)
    turn_y = [[jnp.cos(yaw), all_zero, jnp.sin(yaw)], [all_zero, all_one, all_zero], [-jnp.sin(yaw), all_zero, jnp.cos(yaw)]]
    turn_x = [[all_one, all_zero, all_zero], [all_zero, jnp.cos(pitch), -jnp.sin(pitch)], [all_zero, jnp.sin(pitch), jnp.cos(pitch)]]
    turn_z = [[jnp.cos(roll), -jnp.sin(roll), all_zero], [jnp.sin(roll), jnp.cos(roll), all_zero], [all_zero, all_zero, all_one]]
    rotation = chain(turn_z, chain(turn_x, turn_y))
    flat_rows = [rotation[line][column] for line in range(3) for column in range(3)]
    return jnp.stack(flat_rows + [offset[0], offset[1], offset[2], focal_len, centre_col, centre_row], axis=1)


def forced_pick(key, total, count, wanted):
    perm = jax.random.permutation(key, total).astype(jnp.int32)
    special = jnp.zeros((total,), jnp.int32)
    for value in wanted:
        special = special + (perm == value).astype(jnp.int32)
    scores = jnp.where(special > 0, -1, jnp.arange(total, dtype=jnp.int32))
    order = jnp.argsort(scores, stable=True)
    return perm[order][:count]


def layout(key):
    keys = jax.random.split(jax.random.fold_in(key, 202), 6)
    devices = N_CELL * N_VIEW
    half = N_CELL // 2
    quarter = N_CELL // 4
    stripe_wanted = [1, N_CELL // 2, N_CELL - 1]
    shifts = jax.vmap(lambda subkey: forced_pick(subkey, RCAP * N_CELL, TILE_DEV, stripe_wanted) % N_CELL)(jax.random.split(keys[0], N_VIEW))
    stripes = (jnp.arange(N_CELL, dtype=jnp.int32)[:, None, None] - shifts[None, :, :].astype(jnp.int32)) % N_CELL
    ordered = stripes * TILE_DEV + jnp.arange(TILE_DEV, dtype=jnp.int32)[None, None, :]
    shuffles = jax.vmap(lambda subkey: jax.random.permutation(subkey, TILE_DEV))(jax.random.split(keys[1], devices)).reshape(N_CELL, N_VIEW, TILE_DEV)
    tile_table = jnp.take_along_axis(ordered, shuffles, axis=2).astype(jnp.int32)
    owner_wanted = [1, devices // 2, devices - 1]
    spread_off = (forced_pick(keys[2], CAP * devices, BLK_DEV, owner_wanted) % devices).astype(jnp.int32)
    renderer = jnp.arange(devices, dtype=jnp.int32)[:, None]
    owners = (renderer - spread_off[None, :]) % devices
    block_gid = owners * BLK_DEV + jnp.arange(BLK_DEV, dtype=jnp.int32)[None, :]
    entry_order = jax.vmap(lambda subkey: jax.random.permutation(subkey, BLK_DEV))(jax.random.split(keys[3], devices))
    entry_gid = jnp.take_along_axis(block_gid, entry_order, axis=1)
    slot_total = TILE_DEV * (LIST - 1)
    scores = jax.vmap(lambda subkey: jax.random.permutation(subkey, slot_total))(jax.random.split(keys[4], devices)).astype(jnp.int32)
    full_tile = jax.random.randint(keys[5], (devices, 1), 0, TILE_DEV)
    scores = jnp.where((jnp.arange(slot_total, dtype=jnp.int32) // (LIST - 1))[None, :] == full_tile, -1, scores)
    ranking = jnp.argsort(jnp.argsort(scores, axis=1, stable=True), axis=1, stable=True)
    chosen = (ranking < BLK_DEV - TILE_DEV).astype(jnp.int32)
    counts = 1 + jnp.sum(chosen.reshape(devices, TILE_DEV, LIST - 1), axis=2)
    starts = jnp.cumsum(counts, axis=1) - counts
    depth_pos = jnp.arange(LIST, dtype=jnp.int32)
    positions = starts[:, :, None] + depth_pos[None, None, :]
    is_live = depth_pos[None, None, :] < counts[:, :, None]
    picked = jnp.take_along_axis(entry_gid, jnp.minimum(positions, BLK_DEV - 1).reshape(devices, -1), axis=1).reshape(devices, TILE_DEV, LIST)
    list_table = jnp.where(is_live, picked, -1).astype(jnp.int32).reshape(N_CELL, N_VIEW, TILE_DEV, LIST)
    tile_flat = tile_table.reshape(devices, TILE_DEV)
    entry_pos = jnp.arange(BLK_DEV, dtype=jnp.int32)
    holder = jnp.sum((starts[:, None, :] <= entry_pos[None, :, None]).astype(jnp.int32), axis=2) - 1
    entry_tile = jnp.take_along_axis(tile_flat, holder, axis=1)
    group_of = (jnp.arange(devices, dtype=jnp.int32) % N_VIEW)[:, None]
    shifted = (entry_tile // TILE_DEV - quarter) % N_CELL
    entry_view = 2 * group_of + shifted // half
    entry_x = 16 * (entry_tile % TILE_DEV)
    entry_y = 16 * (shifted % half)
    flat_gid = entry_gid.reshape(-1)
    block_view = jnp.zeros((devices * BLK_DEV,), jnp.int32).at[flat_gid].set(entry_view.reshape(-1))
    block_x = jnp.zeros((devices * BLK_DEV,), jnp.int32).at[flat_gid].set(entry_x.reshape(-1))
    block_y = jnp.zeros((devices * BLK_DEV,), jnp.int32).at[flat_gid].set(entry_y.reshape(-1))
    return (tile_table, list_table, block_view, block_x, block_y)


def draw_cameras(key, part):
    table = camera_table(key)
    return table


def draw_tile_ids(key, part):
    tile_table, list_table, block_view, block_x, block_y = layout(key)
    return tile_table


def draw_tile_blocks(key, part):
    tile_table, list_table, block_view, block_x, block_y = layout(key)
    return list_table


def draw_gauss_params(key, part):
    table = camera_table(key)
    tile_table, list_table, block_view, block_x, block_y = layout(key)
    key = jax.random.fold_in(key, 3)
    keys = jax.random.split(key, 9)
    count = GAUSS
    view_of = jnp.repeat(block_view, GBLK)
    per_gauss = [table[:, number][view_of] for number in range(15)]
    screen_x = jnp.repeat(block_x, GBLK).astype(jnp.float32) + jax.random.uniform(keys[0], (count,), jnp.float32, -3.0, 19.0)
    screen_y = jnp.repeat(block_y, GBLK).astype(jnp.float32) + jax.random.uniform(keys[1], (count,), jnp.float32, -3.0, 19.0)
    depths = jax.random.uniform(keys[2], (count,), jnp.float32, 4.0, 40.0)
    focal_len = per_gauss[12]
    in_camera = [(screen_x - per_gauss[13]) * depths / focal_len, (screen_y - per_gauss[14]) * depths / focal_len, depths]
    relative = [in_camera[line] - per_gauss[9 + line] for line in range(3)]
    world = [per_gauss[column] * relative[0] + per_gauss[3 + column] * relative[1] + per_gauss[6 + column] * relative[2] for column in range(3)]
    spread_px = jnp.exp(jax.random.uniform(keys[3], (count,), jnp.float32, 0.0, math.log(3.0)))
    log_size = jnp.log(spread_px * depths / focal_len)
    log_scales = log_size[None, :] + 0.25 * jax.random.normal(keys[4], (3, count), jnp.float32)
    real_part = jax.random.uniform(keys[5], (1, count), jnp.float32, 1.0, 2.0)
    imag_part = 0.6 * jax.random.normal(keys[6], (3, count), jnp.float32)
    logits = jax.random.uniform(keys[7], (1, count), jnp.float32, -6.0, 2.0)
    spread_sh = jnp.concatenate([jnp.full((3, 1), 0.8, jnp.float32), jnp.full((45, 1), 0.2, jnp.float32)], axis=0)
    harmonic = jax.random.normal(keys[8], (48, count), jnp.float32) * spread_sh
    return jnp.concatenate([jnp.stack(world), log_scales, real_part, imag_part, logits, harmonic], axis=0)


def draw_target(key, part):
    key = jax.random.fold_in(key, 7)
    keys = jax.random.split(key, 3)
    node_rows = ROWS // 16 + 1
    node_cols = IMG_W // 16 + 1
    base = jax.random.uniform(keys[0], (N_VIEW, 1, node_rows, node_cols), jnp.float32, 0.15, 0.7)
    tint = 0.06 * jax.random.normal(keys[1], (N_VIEW, 3, node_rows, node_cols), jnp.float32)
    grain = 0.03 * jax.random.normal(keys[2], (N_VIEW, 3, ROWS, IMG_W), jnp.float32)
    nodes = base + tint
    row_pos = jnp.arange(ROWS, dtype=jnp.int32)
    col_pos = jnp.arange(IMG_W, dtype=jnp.int32)
    row_low = row_pos // 16
    col_low = col_pos // 16
    row_frac = (row_pos % 16).astype(jnp.float32) / 16.0
    col_frac = (col_pos % 16).astype(jnp.float32) / 16.0
    top_rows = nodes[:, :, row_low, :]
    next_rows = nodes[:, :, row_low + 1, :]
    row_mixed = top_rows * (1.0 - row_frac)[:, None] + next_rows * row_frac[:, None]
    left_side = row_mixed[:, :, :, col_low]
    right_side = row_mixed[:, :, :, col_low + 1]
    smooth = left_side * (1.0 - col_frac) + right_side * col_frac
    return jnp.clip(smooth + grain, 0.02, 1.0)


def touch_ends(result, stream_key, smallest, largest):
    extent = result.shape
    index_at = [jax.random.randint(jax.random.fold_in(stream_key, axis), (), 0, extent[axis]) for axis in range(len(extent))]
    result = result.at[tuple(index_at)].set(smallest)
    longest = extent.index(max(extent))
    index_at[longest] = (index_at[longest] + 1) % extent[longest]
    return result.at[tuple(index_at)].set(largest)


def setup_inputs(seed: int = 0) -> dict:
    key_list = jax.random.split(jax.random.key(seed), 7)
    return {
        "gauss_params": draw_gauss_params(jax.random.fold_in(key_list[6], 71), 0),
        "visible": touch_ends((jax.random.randint(key_list[1], (VIEWS, GAUSS), 0, 8) < 7).astype(jnp.int32), jax.random.fold_in(key_list[1], 1), 0, 1),
        "cameras": draw_cameras(jax.random.fold_in(key_list[6], 71), 0),
        "tile_ids": draw_tile_ids(jax.random.fold_in(key_list[6], 71), 0),
        "tile_blocks": draw_tile_blocks(jax.random.fold_in(key_list[6], 71), 0),
        "target": draw_target(jax.random.fold_in(key_list[6], 71), 0),
    }


def harmonics(unit_x, unit_y, unit_z):
    square_x = unit_x * unit_x
    square_y = unit_y * unit_y
    square_z = unit_z * unit_z
    return [0.28209479177387814 + 0.0 * unit_x, -0.4886025119029199 * unit_y, 0.4886025119029199 * unit_z, -0.4886025119029199 * unit_x, 1.0925484305920792 * unit_x * unit_y, -1.0925484305920792 * unit_y * unit_z, 0.31539156525252005 * (2.0 * square_z - square_x - square_y), -1.0925484305920792 * unit_x * unit_z, 0.5462742152960396 * (square_x - square_y), -0.5900435899266435 * unit_y * (3.0 * square_x - square_y), 2.890611442640554 * unit_x * unit_y * unit_z, -0.4570457994644658 * unit_y * (4.0 * square_z - square_x - square_y), 0.3731763325901154 * unit_z * (2.0 * square_z - 3.0 * square_x - 3.0 * square_y), -0.4570457994644658 * unit_x * (4.0 * square_z - square_x - square_y), 1.445305721320277 * unit_z * (square_x - square_y), -0.5900435899266435 * unit_x * (square_x - 3.0 * square_y)]

def project(raw_params, camera, seen_mask):
    entries = [camera[:, number][:, None] for number in range(15)]
    rotation = [[entries[0], entries[1], entries[2]], [entries[3], entries[4], entries[5]], [entries[6], entries[7], entries[8]]]
    offset = [entries[9], entries[10], entries[11]]
    focal_len = entries[12]
    centre_pos = [raw_params[:, number] for number in range(3)]
    in_camera = [rotation[member][0] * centre_pos[0] + rotation[member][1] * centre_pos[1] + rotation[member][2] * centre_pos[2] + offset[member] for member in range(3)]
    depths = in_camera[2]
    screen_x = focal_len * in_camera[0] / depths + entries[13]
    screen_y = focal_len * in_camera[1] / depths + entries[14]
    quaternion = [raw_params[:, 6 + number] for number in range(4)]
    length = jnp.sqrt(quaternion[0] * quaternion[0] + quaternion[1] * quaternion[1] + quaternion[2] * quaternion[2] + quaternion[3] * quaternion[3])
    real_part, imag_x, imag_y, imag_z = [part / length for part in quaternion]
    turn_q = [[1.0 - 2.0 * (imag_y * imag_y + imag_z * imag_z), 2.0 * (imag_x * imag_y - real_part * imag_z), 2.0 * (imag_x * imag_z + real_part * imag_y)], [2.0 * (imag_x * imag_y + real_part * imag_z), 1.0 - 2.0 * (imag_x * imag_x + imag_z * imag_z), 2.0 * (imag_y * imag_z - real_part * imag_x)], [2.0 * (imag_x * imag_z - real_part * imag_y), 2.0 * (imag_y * imag_z + real_part * imag_x), 1.0 - 2.0 * (imag_x * imag_x + imag_y * imag_y)]]
    squares = [jnp.exp(2.0 * raw_params[:, 3 + number]) for number in range(3)]
    jacobian = [[focal_len / depths, 0.0 * depths, -focal_len * in_camera[0] / (depths * depths)], [0.0 * depths, focal_len / depths, -focal_len * in_camera[1] / (depths * depths)]]
    with_cam = [[jacobian[member][0] * rotation[0][column] + jacobian[member][1] * rotation[1][column] + jacobian[member][2] * rotation[2][column] for column in range(3)] for member in range(2)]
    whole = [[with_cam[member][0] * turn_q[0][column] + with_cam[member][1] * turn_q[1][column] + with_cam[member][2] * turn_q[2][column] for column in range(3)] for member in range(2)]
    cov_a = squares[0] * whole[0][0] * whole[0][0] + squares[1] * whole[0][1] * whole[0][1] + squares[2] * whole[0][2] * whole[0][2] + 0.3
    cov_b = squares[0] * whole[0][0] * whole[1][0] + squares[1] * whole[0][1] * whole[1][1] + squares[2] * whole[0][2] * whole[1][2]
    cov_c = squares[0] * whole[1][0] * whole[1][0] + squares[1] * whole[1][1] * whole[1][1] + squares[2] * whole[1][2] * whole[1][2] + 0.3
    determinant = cov_a * cov_c - cov_b * cov_b
    eye_pos = [-(rotation[0][column] * offset[0] + rotation[1][column] * offset[1] + rotation[2][column] * offset[2]) for column in range(3)]
    heading = [centre_pos[column] - eye_pos[column] for column in range(3)]
    distance = jnp.sqrt(heading[0] * heading[0] + heading[1] * heading[1] + heading[2] * heading[2])
    basis = harmonics(heading[0] / distance, heading[1] / distance, heading[2] / distance)
    colours = [jnp.maximum(0.5 + sum((basis[number] * raw_params[:, 11 + 3 * number + channel] for number in range(16))), 0.0) for channel in range(3)]
    opacity = seen_mask / (1.0 + jnp.exp(-raw_params[:, 10]))
    return jnp.stack([screen_x, screen_y, cov_c / determinant, -cov_b / determinant, cov_a / determinant, opacity] + colours, axis=1)

def composite(features, across_x, across_y, log_trans, colour):
    dist_x = across_x[:, :, None] - features[:, 0][:, None, :]
    dist_y = across_y[:, :, None] - features[:, 1][:, None, :]
    exponent = -0.5 * (features[:, 2][:, None, :] * dist_x * dist_x + features[:, 4][:, None, :] * dist_y * dist_y) - features[:, 3][:, None, :] * dist_x * dist_y
    alphas = features[:, 5][:, None, :] * jnp.exp(exponent)
    log_keep = jnp.log1p(-alphas)
    before = jnp.cumsum(log_keep, axis=2) - log_keep
    weights = alphas * jnp.exp(log_trans[:, :, None] + before)
    colour = colour + jnp.einsum('tpg,tcg->tcp', weights, features[:, 6:9], precision=lax.Precision.HIGHEST)
    return (log_trans + lax.optimization_barrier(jnp.sum(log_keep, axis=2)), colour)

def window_taps():
    offsets = jnp.arange(11).astype(jnp.float32) - 5.0
    taps = jnp.exp(-offsets * offsets / 4.5)
    return taps / jnp.sum(taps)

def blur(stack, row_count):
    taps = window_taps()
    columns = stack.shape[-1]
    widths = [(0, 0)] * (stack.ndim - 1) + [(5, 5)]
    wide = jnp.pad(stack, widths)
    across = sum((taps[number] * wide[..., number:number + columns] for number in range(11)))
    return sum((taps[number] * across[..., number:number + row_count, :] for number in range(11)))

def stripe_loss(images, targets, row_count):
    stack = jnp.stack([images, targets, images * images, targets * targets, images * targets])
    blurred = blur(stack, row_count)
    mean_x = blurred[0]
    mean_y = blurred[1]
    var_x = blurred[2] - mean_x * mean_x
    var_y = blurred[3] - mean_y * mean_y
    covar = blurred[4] - mean_x * mean_y
    ssim_map = (2.0 * mean_x * mean_y + 0.0001) * (2.0 * covar + 0.0009) / ((mean_x * mean_x + mean_y * mean_y + 0.0001) * (var_x + var_y + 0.0009))
    inner_x = images[..., 5:5 + row_count, :]
    inner_y = targets[..., 5:5 + row_count, :]
    return 0.8 * lax.optimization_barrier(jnp.mean(jnp.abs(inner_x - inner_y), axis=-3)) + 0.2 * (1.0 - lax.optimization_barrier(jnp.mean(ssim_map, axis=-3)))

def reference(gauss_params, visible, cameras, tile_ids, tile_blocks, target):
    half = N_CELL // 2
    quarter = N_CELL // 4
    blocks_all = gauss_params.shape[1] // GBLK
    param_blocks = gauss_params.reshape(FEAT, blocks_all, GBLK)
    seen_blocks = visible.reshape(VIEWS, blocks_all, GBLK).astype(jnp.float32)
    pixels = jnp.arange(256, dtype=jnp.int32)
    columns = jnp.arange(TILE_DEV, dtype=jnp.int32)
    across_x = (16 * columns[:, None] + pixels[None, :] % 16).astype(jnp.float32)
    images = []
    for group_id in range(N_VIEW):
        tile_list = tile_ids[:, group_id].reshape(-1)
        entry_list = tile_blocks[:, group_id].reshape(-1, LIST)
        by_tile = jnp.zeros((N_CELL * TILE_DEV, LIST), jnp.int32).at[tile_list].set(entry_list).reshape(N_CELL, TILE_DEV, LIST)

        def render_stripe(inputs):
            stripe, entries = inputs
            shifted = (stripe - quarter) % N_CELL
            view_id = 2 * group_id + shifted // half
            row_base = 16 * (shifted % half)
            across_y = jnp.broadcast_to((row_base + pixels // 16).astype(jnp.float32)[None, :], (TILE_DEV, 256))
            camera = jnp.broadcast_to(cameras[view_id][None, :], (TILE_DEV, 15))
            log_trans = jnp.zeros((TILE_DEV, 256), jnp.float32)
            colour = jnp.zeros((TILE_DEV, 3, 256), jnp.float32)
            for number in range(LIST):
                block_ids = entries[:, number]
                is_live = (block_ids >= 0).astype(jnp.float32)
                clipped = jnp.maximum(block_ids, 0)
                raw_params = jnp.moveaxis(param_blocks[:, clipped], 0, 1)
                seen_mask = seen_blocks[view_id, clipped] * is_live[:, None]
                features = project(raw_params, camera, seen_mask)
                log_trans, colour = composite(features, across_x, across_y, log_trans, colour)
            return colour
        colours = lax.map(render_stripe, (jnp.arange(N_CELL, dtype=jnp.int32), by_tile))
        images.append(colours.reshape(N_CELL, TILE_DEV, 3, 16, 16).transpose(2, 0, 3, 1, 4).reshape(3, ROWS, IMG_W))
    image = jnp.stack(images)
    moved = IMG_H // 2
    rolled_image = jnp.roll(image, -moved, axis=2)
    rolled_target = jnp.roll(target, -moved, axis=2)
    split_image = rolled_image.reshape(N_VIEW, 3, 2, IMG_H, IMG_W).transpose(0, 2, 1, 3, 4)
    split_target = rolled_target.reshape(N_VIEW, 3, 2, IMG_H, IMG_W).transpose(0, 2, 1, 3, 4)
    widths = [(0, 0), (0, 0), (0, 0), (5, 5), (0, 0)]
    loss_parts = stripe_loss(jnp.pad(split_image, widths), jnp.pad(split_target, widths), IMG_H)
    loss_map = jnp.roll(loss_parts.reshape(N_VIEW, ROWS, IMG_W), moved, axis=1)
    return (image, loss_map)
```

```python
import functools

import jax
import jax.numpy as jnp
from jax import lax
from jax.experimental import pallas as pl
from jax.experimental.pallas import tpu as pltpu
from jax.sharding import PartitionSpec as P

MESH = pl.DeviceIdType.MESH
F32 = jnp.float32
BF16 = jnp.bfloat16
LOG2E = 1.4426950408889634
NEG = -1e30
NB = 150
NBP = 152
CELLS = 128
TILES = 120


def dot00(left, right):
    return lax.dot_general(left, right, (((0,), (0,)), ((), ())), preferred_element_type=F32)


def dot10(left, right):
    return lax.dot_general(left, right, (((1,), (0,)), ((), ())), preferred_element_type=F32)


def pieces(value):
    high = value.astype(BF16)
    rest = value - high.astype(F32)
    mid = rest.astype(BF16)
    low = (rest - mid.astype(F32)).astype(BF16)
    return high, mid, low


def iota(shape, dim):
    return lax.broadcasted_iota(jnp.int32, shape, dim)


def quotient(value, divisor):
    return ((value.astype(F32) + 0.5) * (1.0 / divisor)).astype(jnp.int32)


def harmonics(ux, uy, uz):
    xx, yy, zz = ux * ux, uy * uy, uz * uz
    return [
        None,
        -0.4886025119029199 * uy,
        0.4886025119029199 * uz,
        -0.4886025119029199 * ux,
        1.0925484305920792 * ux * uy,
        -1.0925484305920792 * uy * uz,
        0.31539156525252005 * (2.0 * zz - xx - yy),
        -1.0925484305920792 * ux * uz,
        0.5462742152960396 * (xx - yy),
        -0.5900435899266435 * uy * (3.0 * xx - yy),
        2.890611442640554 * ux * uy * uz,
        -0.4570457994644658 * uy * (4.0 * zz - xx - yy),
        0.3731763325901154 * uz * (2.0 * zz - 3.0 * xx - 3.0 * yy),
        -0.4570457994644658 * ux * (4.0 * zz - xx - yy),
        1.445305721320277 * uz * (xx - yy),
        -0.5900435899266435 * ux * (xx - 3.0 * yy),
    ]


def project_chunk(raw, seen, cam, view):
    def pick(entry):
        return jnp.where(
            view < 1.5,
            jnp.where(view < 0.5, cam[0, entry], cam[1, entry]),
            jnp.where(view < 2.5, cam[2, entry], cam[3, entry]),
        )

    e = [pick(entry) for entry in range(15)]
    rot = [e[0:3], e[3:6], e[6:9]]
    off = e[9:12]
    focal = e[12]
    pos = [raw(n) for n in range(3)]
    pc = [rot[m][0] * pos[0] + rot[m][1] * pos[1] + rot[m][2] * pos[2] + off[m] for m in range(3)]
    inv_z = 1.0 / pc[2]
    fz = focal * inv_z
    sx = focal * pc[0] / pc[2] + e[13]
    sy = focal * pc[1] / pc[2] + e[14]
    q = [raw(6 + n) for n in range(4)]
    scale = 1.0 / jnp.sqrt(q[0] * q[0] + q[1] * q[1] + q[2] * q[2] + q[3] * q[3])
    r, x, y, z = [part * scale for part in q]
    turn = [
        [1.0 - 2.0 * (y * y + z * z), 2.0 * (x * y - r * z), 2.0 * (x * z + r * y)],
        [2.0 * (x * y + r * z), 1.0 - 2.0 * (x * x + z * z), 2.0 * (y * z - r * x)],
        [2.0 * (x * z - r * y), 2.0 * (y * z + r * x), 1.0 - 2.0 * (x * x + y * y)],
    ]
    sq = [jnp.exp(2.0 * raw(3 + n)) for n in range(3)]
    jz = [-fz * pc[0] * inv_z, -fz * pc[1] * inv_z]
    cams = [[fz * rot[m][k] + jz[m] * rot[2][k] for k in range(3)] for m in range(2)]
    w = [
        [cams[m][0] * turn[0][k] + cams[m][1] * turn[1][k] + cams[m][2] * turn[2][k] for k in range(3)]
        for m in range(2)
    ]
    s0 = [sq[k] * w[0][k] for k in range(3)]
    cov_a = s0[0] * w[0][0] + s0[1] * w[0][1] + s0[2] * w[0][2] + 0.3
    cov_b = s0[0] * w[1][0] + s0[1] * w[1][1] + s0[2] * w[1][2]
    cov_c = sq[0] * w[1][0] * w[1][0] + sq[1] * w[1][1] * w[1][1] + sq[2] * w[1][2] * w[1][2] + 0.3
    inv_det = 1.0 / (cov_a * cov_c - cov_b * cov_b)
    eye = [-(rot[0][k] * off[0] + rot[1][k] * off[1] + rot[2][k] * off[2]) for k in range(3)]
    head = [pos[k] - eye[k] for k in range(3)]
    inv_len = 1.0 / jnp.sqrt(head[0] * head[0] + head[1] * head[1] + head[2] * head[2])
    basis = harmonics(head[0] * inv_len, head[1] * inv_len, head[2] * inv_len)
    colours = []
    for k in range(3):
        total = 0.5 + 0.28209479177387814 * raw(11 + k)
        for j in range(1, 16):
            total = total + basis[j] * raw(11 + 3 * j + k)
        colours.append(jnp.maximum(total, 0.0))
    log_o = jnp.maximum(-LOG2E * jnp.log1p(jnp.exp(-raw(10))), NEG)
    log_o = jnp.where(seen > 0, log_o, NEG)
    return [
        sx,
        sy,
        (-0.5 * LOG2E) * (cov_c * inv_det),
        LOG2E * (cov_b * inv_det),
        (-0.5 * LOG2E) * (cov_a * inv_det),
        log_o,
    ] + colours


def kernel(
    params,
    visible,
    cam,
    tile_ids,
    tile_blocks,
    target,
    image_out,
    loss_out,
    par_s,
    vis_s,
    tid_s,
    req,
    rreq,
    pick1,
    pick2,
    view_s,
    feat,
    grid_f,
    px_s,
    sbuf,
    rbuf,
    s2buf,
    r2buf,
    tpad,
    ipad,
    vert,
    blur_t,
    blur_i,
    load_sem,
    req_send,
    req_recv,
    halo_send,
    halo_recv,
    one_send,
    one_recv,
    two_send,
    two_recv,
    own_sem,
):
    my_c = lax.axis_index("cell")
    my_v = lax.axis_index("view")
    me_slot = my_v * CELLS + my_c

    barrier = pltpu.get_barrier_semaphore()

    def greet(k, carry):
        cell = lax.rem(my_c + k, CELLS)
        pl.semaphore_signal(barrier, inc=1, device_id=(cell, my_v), device_id_type=MESH)
        pl.semaphore_signal(barrier, inc=1, device_id=(cell, 1 - my_v), device_id_type=MESH)
        return carry

    pl.semaphore_signal(barrier, inc=1, device_id=(my_c, 1 - my_v), device_id_type=MESH)
    lax.fori_loop(1, CELLS, greet, 0)

    par_s[:, NB:NBP, :] = jnp.zeros((59, NBP - NB, 128), F32)
    vis_s[:, NB:NBP, :] = jnp.zeros((4, NBP - NB, 128), jnp.int32)

    def load(b, carry):
        lanes = pl.ds(pl.multiple_of(b * 128, 128), 128)
        pltpu.make_async_copy(params.at[:, lanes], par_s.at[:, b, :], load_sem.at[0]).start()
        pltpu.make_async_copy(visible.at[:, lanes], vis_s.at[:, b, :], load_sem.at[1]).start()
        return carry

    lax.fori_loop(0, NB, load, 0)

    tid_s[...] = jnp.full((8, 128), -1.0, F32)
    tid_s[0:1, 0:TILES] = tile_ids[...].astype(F32)
    tid = jnp.transpose(jnp.broadcast_to(tid_s[0:1, :], (128, 128)))[0:TILES, 0:1].astype(jnp.int32)
    stripe = quotient(tid, TILES)
    column = tid - TILES * stripe
    lane2 = iota((TILES, 256), 1)
    hits = []
    local = []
    for entry in range(2):
        block = tile_blocks[:, entry : entry + 1]
        owner = quotient(jnp.maximum(block, 0), NB)
        cell = owner // 2
        slot = (owner - 2 * cell) * CELLS + cell
        hits.append((jnp.where(block >= 0, slot, -1) == lane2).astype(F32))
        local.append((block - NB * owner + 1).astype(F32))
    by_stripe = (stripe == iota((TILES, 128), 1)).astype(F32)
    lb_row = jnp.sum(hits[0] * local[0] + hits[1] * local[1], axis=0, keepdims=True) - 1.0
    tl_row = jnp.sum((hits[0] + hits[1]) * tid.astype(F32), axis=0, keepdims=True)
    col_row = jnp.sum(by_stripe * (column + 1).astype(F32), axis=0, keepdims=True) - 1.0
    sub = iota((128, 128), 0)
    for part in range(2):
        lanes = slice(128 * part, 128 * (part + 1))
        text = jnp.where(
            sub < 32, lb_row[:, lanes], jnp.where(sub < 64, tl_row[:, lanes], col_row)
        )
        req[lanes, 0, :] = jnp.transpose(text).astype(jnp.int32)
    stripe_hot = by_stripe.astype(BF16)
    pick1[...] = dot00(stripe_hot, hits[0].astype(BF16)).astype(BF16)
    pick2[...] = dot00(stripe_hot, hits[1].astype(BF16)).astype(BF16)
    tpad[:, 8:24, :] = target[...]

    pl.semaphore_wait(barrier, 2 * CELLS - 1)

    def exchange(src, dst, rows, send, recv, view, first):
        def go(k, carry):
            cell = lax.rem(my_c + k, CELLS)
            pltpu.make_async_remote_copy(
                src_ref=src.at[view * CELLS + cell, pl.ds(0, rows)],
                dst_ref=dst.at[me_slot, pl.ds(0, rows)],
                send_sem=send,
                recv_sem=recv,
                device_id=(cell, view),
                device_id_type=MESH,
            ).start()
            return carry

        lax.fori_loop(first, CELLS, go, 0)

    def settle(ref, count, rows, sem):
        part = ref.at[pl.ds(0, count), pl.ds(0, rows)]
        pltpu.make_async_copy(part, part, sem).wait()

    def own(src, dst):
        copy = pltpu.make_async_copy(src, dst, own_sem)
        copy.start()
        copy.wait()

    exchange(req, rreq, 1, req_send, req_recv, my_v, 1)
    exchange(req, rreq, 1, req_send, req_recv, 1 - my_v, 0)

    above = lax.rem(my_c + CELLS - 1, CELLS)
    below = lax.rem(my_c + 1, CELLS)

    def halo(buf, number):
        up = pltpu.make_async_remote_copy(
            src_ref=buf.at[:, pl.ds(8, 8), :],
            dst_ref=buf.at[:, pl.ds(24, 8), :],
            send_sem=halo_send.at[2 * number],
            recv_sem=halo_recv.at[2 * number],
            device_id=(above, my_v),
            device_id_type=MESH,
        )
        down = pltpu.make_async_remote_copy(
            src_ref=buf.at[:, pl.ds(16, 8), :],
            dst_ref=buf.at[:, pl.ds(0, 8), :],
            send_sem=halo_send.at[2 * number + 1],
            recv_sem=halo_recv.at[2 * number + 1],
            device_id=(below, my_v),
            device_id_type=MESH,
        )
        up.start()
        down.start()
        return up, down

    target_halo = halo(tpad, 0)
    own(req.at[me_slot], rreq.at[me_slot])
    settle(rreq, 255, 1, req_recv)

    asked = rreq[:, 0, :].astype(F32)
    turned = jnp.concatenate(
        [jnp.transpose(asked[0:128]), jnp.transpose(asked[128:256])], axis=1
    )
    want = turned[0:1, :].astype(jnp.int32)
    tile = turned[32:33, :].astype(jnp.int32)
    cols_in = jnp.where(my_v == 0, turned[64:65, 0:128], turned[64:65, 128:256]).astype(jnp.int32)
    t_stripe = quotient(tile, TILES)
    t_col = tile - TILES * t_stripe
    place = t_stripe - CELLS // 4
    place = jnp.where(place < 0, place + CELLS, place)
    side = (place >= CELLS // 2).astype(jnp.int32)
    anchor_x = (16 * t_col).astype(F32)
    anchor_y = (16 * (place - (CELLS // 2) * side)).astype(F32)
    view_d = (2 * (iota((1, 256), 1) // CELLS) + side).astype(F32)
    hot = (iota((NBP, 256), 0) == want).astype(F32)
    view_s[...] = jnp.broadcast_to(jnp.sum(hot * view_d, axis=1, keepdims=True), (NBP, 128))
    hot16 = hot.astype(BF16)

    pltpu.make_async_copy(par_s.at[:, pl.ds(0, NB), :], par_s.at[:, pl.ds(0, NB), :], load_sem.at[0]).wait()
    pltpu.make_async_copy(vis_s.at[:, pl.ds(0, NB), :], vis_s.at[:, pl.ds(0, NB), :], load_sem.at[1]).wait()

    def project(i, carry):
        rows = pl.ds(pl.multiple_of(8 * i, 8), 8)
        view = view_s[rows, :]
        seen = jnp.where(
            view < 1.5,
            jnp.where(view < 0.5, vis_s[0, rows, :], vis_s[1, rows, :]),
            jnp.where(view < 2.5, vis_s[2, rows, :], vis_s[3, rows, :]),
        )
        found = project_chunk(lambda f: par_s[f, rows, :], seen, cam, view)
        inside = iota((8, 128), 0) + 8 * i < NB
        for f in range(9):
            feat[f, rows, :] = jnp.where(inside, found[f], 0.0)
        return carry

    lax.fori_loop(0, NBP // 8, project, 0)

    live = want >= 0
    for f in range(9):
        high, mid, low = pieces(feat[f])
        got = (dot00(low, hot16) + dot00(mid, hot16)) + dot00(high, hot16)
        if f == 0:
            got = got - anchor_x
        if f == 1:
            got = got - anchor_y
        if f == 5:
            got = jnp.where(live, got, NEG)
        grid_f[0, f] = got[:, 0:128]
        grid_f[1, f] = got[:, 128:256]

    sub8 = iota((8, 128), 0).astype(F32)

    def render(view):
        for quarter in range(4):

            def blend(g, state):
                state = list(state)
                row = [
                    jnp.broadcast_to(grid_f[view, f, pl.ds(g, 1), :], (8, 128)) for f in range(9)
                ]
                dx = [sub8 - row[0], (sub8 + 8.0) - row[0]]
                lead = [row[2] * d * d + row[5] for d in dx]
                cross = [row[3] * d for d in dx]
                for line in range(4):
                    dy = (4.0 * quarter + line) - row[1]
                    bend = row[4] * dy
                    for half in range(2):
                        at = 4 * (2 * line + half)
                        alpha = jnp.exp2(lead[half] + dy * (cross[half] + bend))
                        weight = alpha * state[at + 3]
                        state[at] = state[at] + weight * row[6]
                        state[at + 1] = state[at + 1] + weight * row[7]
                        state[at + 2] = state[at + 2] + weight * row[8]
                        state[at + 3] = state[at + 3] - weight
                return tuple(state)

            zero = jnp.zeros((8, 128), F32)
            one = jnp.ones((8, 128), F32)
            state = lax.fori_loop(0, 128, blend, (zero, zero, zero, one) * 8)
            for at in range(8):
                start = 64 * (quarter % 2) + 8 * at
                for k in range(4):
                    px_s[2 * k + quarter // 2, start : start + 8, :] = state[4 * at + k]
        rows = pl.ds(pl.multiple_of(view * CELLS, CELLS), CELLS)
        for k in range(8):
            sbuf[rows, k, :] = jnp.transpose(px_s[k])

    render(my_v)
    exchange(sbuf, rbuf, 8, one_send, one_recv, my_v, 1)
    own(sbuf.at[me_slot], rbuf.at[me_slot])
    render(1 - my_v)
    exchange(sbuf, rbuf, 8, one_send, one_recv, 1 - my_v, 0)

    taps = [0.0] * 6
    total = sum(2.718281828459045 ** (-(k * k) / 4.5) for k in range(-5, 6))
    for k in range(6):
        taps[k] = 2.718281828459045 ** (-(k * k) / 4.5) / total

    spot = lax.rem(my_c + CELLS - CELLS // 4, CELLS // 2)
    keep_top = jnp.where(spot != 0, 1.0, 0.0)
    keep_bottom = jnp.where(spot != CELLS // 2 - 1, 1.0, 0.0)

    def down_columns(terms):
        totals = [taps[0] * v for v in terms(0)]
        for k in range(1, 6):
            lower, upper = terms(-k), terms(k)
            totals = [t + taps[k] * (a + b) for t, a, b in zip(totals, lower, upper)]
        return totals

    def along_rows(count, out):
        def go(i, carry):
            plane = i // 2
            rows = pl.ds(pl.multiple_of(8 * (i % 2), 8), 8)
            x = vert[plane, rows, :]
            acc = taps[0] * x
            for k in range(1, 6):
                acc = acc + taps[k] * (pltpu.roll(x, k, 1) + pltpu.roll(x, 2048 - k, 1))
            out[plane, rows, :] = acc[:, 0:1920]
            return carry

        lax.fori_loop(0, 2 * count, go, 0)

    for copy in target_halo:
        copy.wait()
    tpad[:, 0:8, :] = tpad[:, 0:8, :] * keep_top
    tpad[:, 24:32, :] = tpad[:, 24:32, :] * keep_bottom
    for plane in range(9):
        vert[plane, :, 1920:2048] = jnp.zeros((16, 128), F32)

    def target_columns(j, carry):
        lanes = pl.ds(pl.multiple_of(128 * j, 128), 128)
        for ch in range(3):

            def terms(k):
                t = tpad[ch, 8 + k : 24 + k, lanes]
                return [t, t * t]

            found = down_columns(terms)
            vert[ch, :, lanes] = found[0]
            vert[3 + ch, :, lanes] = found[1]
        return carry

    lax.fori_loop(0, 15, target_columns, 0)
    along_rows(6, blur_t)

    settle(req, 255, 1, req_send)
    settle(rbuf, 255, 8, one_recv)
    hot1 = pick1[...]
    hot2 = pick2[...]

    def both(k):
        parts = pieces(rbuf[:, k, :])
        first = (dot10(hot1, parts[2]) + dot10(hot1, parts[1])) + dot10(hot1, parts[0])
        if k >= 6:
            return first, None
        second = (dot10(hot2, parts[2]) + dot10(hot2, parts[1])) + dot10(hot2, parts[0])
        return first, second

    clear = [both(6)[0], both(7)[0]]
    for k in range(6):
        first, second = both(k)
        s2buf[:, k, :] = first + clear[k % 2] * second

    def exchange2(k, carry):
        cell = lax.rem(my_c + k, CELLS)
        pltpu.make_async_remote_copy(
            src_ref=s2buf.at[cell, pl.ds(0, 6)],
            dst_ref=r2buf.at[my_c, pl.ds(0, 6)],
            send_sem=two_send,
            recv_sem=two_recv,
            device_id=(cell, my_v),
            device_id_type=MESH,
        ).start()
        return carry

    lax.fori_loop(1, CELLS, exchange2, 0)
    own(s2buf.at[my_c], r2buf.at[my_c])
    settle(sbuf, 255, 8, one_send)
    settle(r2buf, 127, 6, two_recv)

    hot_col = (iota((TILES, 128), 0) == cols_in).astype(BF16)
    sub_b = iota((15, 8, 128), 1)
    lane_b = iota((15, 8, 128), 2) // 16
    for k in range(6):
        parts = pieces(r2buf[:, k, :])
        found = (dot10(hot_col, parts[2]) + dot10(hot_col, parts[1])) + dot10(hot_col, parts[0])
        cube = found.reshape(15, 8, 128)
        for bit in (1, 2, 4):
            sub_bit = (sub_b & bit) != 0
            lane_bit = (lane_b & bit) != 0
            from_up = pltpu.roll(pltpu.roll(cube, bit, 1), 128 - 16 * bit, 2)
            from_down = pltpu.roll(pltpu.roll(cube, 8 - bit, 1), 16 * bit, 2)
            cube = jnp.where(sub_bit == lane_bit, cube, jnp.where(sub_bit, from_up, from_down))
        top = 8 + 8 * (k % 2)
        for j in range(15):
            ipad[k // 2, top : top + 8, 128 * j : 128 * (j + 1)] = cube[j]

    image_halo = halo(ipad, 1)
    image_out[...] = ipad[:, 8:24, :]
    settle(s2buf, 127, 6, two_send)
    for copy in image_halo:
        copy.wait()
    ipad[:, 0:8, :] = ipad[:, 0:8, :] * keep_top
    ipad[:, 24:32, :] = ipad[:, 24:32, :] * keep_bottom

    def image_columns(j, carry):
        lanes = pl.ds(pl.multiple_of(128 * j, 128), 128)
        for ch in range(3):

            def terms(k):
                x = ipad[ch, 8 + k : 24 + k, lanes]
                return [x, x * x, x * tpad[ch, 8 + k : 24 + k, lanes]]

            found = down_columns(terms)
            for n in range(3):
                vert[3 * n + ch, :, lanes] = found[n]
        return carry

    lax.fori_loop(0, 15, image_columns, 0)
    along_rows(9, blur_i)

    def finish(j, carry):
        lanes = pl.ds(pl.multiple_of(128 * j, 128), 128)
        apart = jnp.zeros((16, 128), F32)
        alike = jnp.zeros((16, 128), F32)
        for ch in range(3):
            mx, sxx, sxy = [blur_i[3 * n + ch, :, lanes] for n in range(3)]
            my, syy = blur_t[ch, :, lanes], blur_t[3 + ch, :, lanes]
            mxx, myy, mxy = mx * mx, my * my, mx * my
            above_line = (2.0 * mxy + 0.0001) * (2.0 * (sxy - mxy) + 0.0009)
            below_line = (mxx + myy + 0.0001) * ((sxx - mxx) + (syy - myy) + 0.0009)
            alike = alike + above_line / below_line
            apart = apart + jnp.abs(ipad[ch, 8:24, lanes] - tpad[ch, 8:24, lanes])
        loss_out[:, lanes] = 0.8 * (apart * (1.0 / 3.0)) + 0.2 * (1.0 - alike * (1.0 / 3.0))
        return carry

    lax.fori_loop(0, 15, finish, 0)


def local(gauss_params, visible, cameras, tile_ids, tile_blocks, target):
    vmem = pl.BlockSpec(memory_space=pltpu.VMEM)
    hbm = pl.BlockSpec(memory_space=pl.ANY)
    dma = pltpu.SemaphoreType.DMA
    image, loss = pl.pallas_call(
        kernel,
        out_shape=(
            jax.ShapeDtypeStruct((3, 16, 1920), F32),
            jax.ShapeDtypeStruct((16, 1920), F32),
        ),
        in_specs=[hbm, hbm, pl.BlockSpec(memory_space=pltpu.SMEM), vmem, vmem, vmem],
        out_specs=(vmem, vmem),
        scratch_shapes=[
            pltpu.VMEM((59, NBP, 128), F32),
            pltpu.VMEM((4, NBP, 128), jnp.int32),
            pltpu.VMEM((8, 128), F32),
            pltpu.VMEM((256, 1, 128), jnp.int32),
            pltpu.VMEM((256, 1, 128), jnp.int32),
            pltpu.VMEM((128, 256), BF16),
            pltpu.VMEM((128, 256), BF16),
            pltpu.VMEM((NBP, 128), F32),
            pltpu.VMEM((9, NBP, 128), F32),
            pltpu.VMEM((2, 9, 128, 128), F32),
            pltpu.VMEM((8, 128, 128), F32),
            pltpu.VMEM((256, 8, 128), F32),
            pltpu.VMEM((256, 8, 128), F32),
            pltpu.VMEM((128, 8, 128), F32),
            pltpu.VMEM((128, 8, 128), F32),
            pltpu.VMEM((3, 32, 1920), F32),
            pltpu.VMEM((3, 32, 1920), F32),
            pltpu.VMEM((9, 16, 2048), F32),
            pltpu.VMEM((6, 16, 1920), F32),
            pltpu.VMEM((9, 16, 1920), F32),
            dma((2,)),
            dma,
            dma,
            dma((4,)),
            dma((4,)),
            dma,
            dma,
            dma,
            dma,
            dma,
        ],
        compiler_params=pltpu.CompilerParams(
            collective_id=0, has_side_effects=True, vmem_limit_bytes=48 << 20
        ),
    )(gauss_params, visible, cameras, tile_ids[0], tile_blocks[0, 0], target[0])
    return (image[None], loss[None])


def solution(mesh):
    return jax.shard_map(
        local,
        mesh=mesh,
        in_specs=(
            P(None, ("cell", "view")),
            P(None, ("cell", "view")),
            P(),
            P("cell", "view", None),
            P("cell", "view", None, None),
            P("view", None, "cell", None),
        ),
        out_specs=(P("view", None, "cell", None), P("view", "cell", None)),
        check_vma=False,
    )
```

```python
import functools

import jax
import jax.numpy as jnp
from jax import lax
from jax.experimental import pallas as pl
from jax.experimental.pallas import tpu as pltpu
from jax.sharding import PartitionSpec as P

MESH = pl.DeviceIdType.MESH
F32 = jnp.float32
BF16 = jnp.bfloat16
LOG2E = 1.4426950408889634
NEG = -1e30
NB = 150
NBP = 152
CELLS = 128
TILES = 120


def dot00(left, right):
    return lax.dot_general(left, right, (((0,), (0,)), ((), ())), preferred_element_type=F32)


def dot10(left, right):
    return lax.dot_general(left, right, (((1,), (0,)), ((), ())), preferred_element_type=F32)


def pieces(value):
    high = value.astype(BF16)
    rest = value - high.astype(F32)
    mid = rest.astype(BF16)
    low = (rest - mid.astype(F32)).astype(BF16)
    return high, mid, low


def iota(shape, dim):
    return lax.broadcasted_iota(jnp.int32, shape, dim)


def quotient(value, divisor):
    return ((value.astype(F32) + 0.5) * (1.0 / divisor)).astype(jnp.int32)


def harmonics(ux, uy, uz):
    xx, yy, zz = ux * ux, uy * uy, uz * uz
    return [
        None,
        -0.4886025119029199 * uy,
        0.4886025119029199 * uz,
        -0.4886025119029199 * ux,
        1.0925484305920792 * ux * uy,
        -1.0925484305920792 * uy * uz,
        0.31539156525252005 * (2.0 * zz - xx - yy),
        -1.0925484305920792 * ux * uz,
        0.5462742152960396 * (xx - yy),
        -0.5900435899266435 * uy * (3.0 * xx - yy),
        2.890611442640554 * ux * uy * uz,
        -0.4570457994644658 * uy * (4.0 * zz - xx - yy),
        0.3731763325901154 * uz * (2.0 * zz - 3.0 * xx - 3.0 * yy),
        -0.4570457994644658 * ux * (4.0 * zz - xx - yy),
        1.445305721320277 * uz * (xx - yy),
        -0.5900435899266435 * ux * (xx - 3.0 * yy),
    ]


def project_chunk(raw, seen, cam, view):
    def pick(entry):
        return jnp.where(
            view < 1.5,
            jnp.where(view < 0.5, cam[0, entry], cam[1, entry]),
            jnp.where(view < 2.5, cam[2, entry], cam[3, entry]),
        )

    e = [pick(entry) for entry in range(15)]
    rot = [e[0:3], e[3:6], e[6:9]]
    off = e[9:12]
    focal = e[12]
    pos = [raw(n) for n in range(3)]
    pc = [rot[m][0] * pos[0] + rot[m][1] * pos[1] + rot[m][2] * pos[2] + off[m] for m in range(3)]
    inv_z = 1.0 / pc[2]
    fz = focal * inv_z
    sx = focal * pc[0] / pc[2] + e[13]
    sy = focal * pc[1] / pc[2] + e[14]
    q = [raw(6 + n) for n in range(4)]
    scale = 1.0 / jnp.sqrt(q[0] * q[0] + q[1] * q[1] + q[2] * q[2] + q[3] * q[3])
    r, x, y, z = [part * scale for part in q]
    turn = [
        [1.0 - 2.0 * (y * y + z * z), 2.0 * (x * y - r * z), 2.0 * (x * z + r * y)],
        [2.0 * (x * y + r * z), 1.0 - 2.0 * (x * x + z * z), 2.0 * (y * z - r * x)],
        [2.0 * (x * z - r * y), 2.0 * (y * z + r * x), 1.0 - 2.0 * (x * x + y * y)],
    ]
    sq = [jnp.exp(2.0 * raw(3 + n)) for n in range(3)]
    jz = [-fz * pc[0] * inv_z, -fz * pc[1] * inv_z]
    cams = [[fz * rot[m][k] + jz[m] * rot[2][k] for k in range(3)] for m in range(2)]
    w = [
        [cams[m][0] * turn[0][k] + cams[m][1] * turn[1][k] + cams[m][2] * turn[2][k] for k in range(3)]
        for m in range(2)
    ]
    s0 = [sq[k] * w[0][k] for k in range(3)]
    cov_a = s0[0] * w[0][0] + s0[1] * w[0][1] + s0[2] * w[0][2] + 0.3
    cov_b = s0[0] * w[1][0] + s0[1] * w[1][1] + s0[2] * w[1][2]
    cov_c = sq[0] * w[1][0] * w[1][0] + sq[1] * w[1][1] * w[1][1] + sq[2] * w[1][2] * w[1][2] + 0.3
    inv_det = 1.0 / (cov_a * cov_c - cov_b * cov_b)
    eye = [-(rot[0][k] * off[0] + rot[1][k] * off[1] + rot[2][k] * off[2]) for k in range(3)]
    head = [pos[k] - eye[k] for k in range(3)]
    inv_len = 1.0 / jnp.sqrt(head[0] * head[0] + head[1] * head[1] + head[2] * head[2])
    basis = harmonics(head[0] * inv_len, head[1] * inv_len, head[2] * inv_len)
    colours = []
    for k in range(3):
        total = 0.5 + 0.28209479177387814 * raw(11 + k)
        for j in range(1, 16):
            total = total + basis[j] * raw(11 + 3 * j + k)
        colours.append(jnp.maximum(total, 0.0))
    log_o = jnp.maximum(-LOG2E * jnp.log1p(jnp.exp(-raw(10))), NEG)
    log_o = jnp.where(seen > 0, log_o, NEG)
    return [
        sx,
        sy,
        (-0.5 * LOG2E) * (cov_c * inv_det),
        LOG2E * (cov_b * inv_det),
        (-0.5 * LOG2E) * (cov_a * inv_det),
        log_o,
    ] + colours


def steps(first, last, body):
    def eight(i, carry):
        for n in range(8):
            body(first + 8 * i + n)
        return carry

    whole = (last - first) // 8
    lax.fori_loop(0, whole, eight, 0)
    for k in range(first + 8 * whole, last):
        body(k)


def kernel(
    params,
    visible,
    cam,
    tile_ids,
    tile_blocks,
    target,
    image_out,
    loss_out,
    par_s,
    vis_s,
    tid_i,
    blk_i,
    list_s,
    pick,
    req,
    rreq,
    view_s,
    feat,
    grid_f,
    px_s,
    sbuf0,
    sbuf1,
    rbuf0,
    rbuf1,
    s2buf0,
    s2buf1,
    r2buf0,
    r2buf1,
    tpad,
    ipad,
    vert,
    blur_t,
    blur_i,
    load_sem,
    small_sem,
    req_send,
    req_recv,
    halo_send,
    halo_recv,
    one_send,
    one_recv,
    two_send,
    two_recv,
    own_sem,
):
    my_c = lax.axis_index("cell")
    my_v = lax.axis_index("view")
    me_slot = my_v * CELLS + my_c

    barrier = pltpu.get_barrier_semaphore()

    small = [
        pltpu.make_async_copy(tile_ids, tid_i, small_sem.at[0]),
        pltpu.make_async_copy(tile_blocks, blk_i, small_sem.at[1]),
        pltpu.make_async_copy(target, tpad.at[:, pl.ds(8, 16), :], small_sem.at[2]),
    ]
    for copy in small:
        copy.start()

    def greet(k):
        cell = lax.rem(my_c + k, CELLS)
        pl.semaphore_signal(barrier, inc=1, device_id=(cell, my_v), device_id_type=MESH)
        pl.semaphore_signal(barrier, inc=1, device_id=(cell, 1 - my_v), device_id_type=MESH)

    pl.semaphore_signal(barrier, inc=1, device_id=(my_c, 1 - my_v), device_id_type=MESH)
    steps(1, CELLS, greet)

    par_s[:, NB:NBP, :] = jnp.zeros((59, NBP - NB, 128), F32)
    vis_s[:, NB:NBP, :] = jnp.zeros((4, NBP - NB, 128), jnp.int32)

    def load(b, carry):
        lanes = pl.ds(pl.multiple_of(b * 128, 128), 128)
        pltpu.make_async_copy(params.at[:, lanes], par_s.at[:, b, :], load_sem.at[0]).start()
        pltpu.make_async_copy(visible.at[:, lanes], vis_s.at[:, b, :], load_sem.at[1]).start()
        return carry

    lax.fori_loop(0, NB, load, 0)

    list_s[...] = jnp.full((8, 128), -1.0, F32)
    small[0].wait()
    small[1].wait()
    list_s[0:1, 0:TILES] = tid_i[...].astype(F32)
    list_s[1:3, 0:TILES] = blk_i[...].astype(F32)
    lists = jnp.transpose(list_s[...])[0:TILES].astype(jnp.int32)
    tid = lists[:, 0:1]
    stripe = quotient(tid, TILES)
    column = tid - TILES * stripe
    lane2 = iota((TILES, 256), 1)
    hits = []
    local = []
    for entry in range(2):
        block = lists[:, 1 + entry : 2 + entry]
        owner = quotient(jnp.maximum(block, 0), NB)
        cell = owner // 2
        slot = (owner - 2 * cell) * CELLS + cell
        slot = jnp.where(block >= 0, slot, -1)
        hits.append((slot == lane2).astype(F32))
        local.append((block - NB * owner + 1).astype(F32))
    by_stripe = (stripe == iota((TILES, 128), 1)).astype(F32)
    lb_row = jnp.sum(hits[0] * local[0] + hits[1] * local[1], axis=0, keepdims=True) - 1.0
    tl_row = jnp.sum((hits[0] + hits[1]) * tid.astype(F32), axis=0, keepdims=True)
    col_row = jnp.sum(by_stripe * (column + 1).astype(F32), axis=0, keepdims=True) - 1.0
    sub = iota((128, 128), 0)
    for part in range(2):
        lanes = slice(128 * part, 128 * (part + 1))
        text = jnp.where(
            sub < 32, lb_row[:, lanes], jnp.where(sub < 64, tl_row[:, lanes], col_row)
        )
        req[lanes, 0, :] = jnp.transpose(text).astype(jnp.int32)
    stripe_hot = by_stripe.astype(BF16)
    for entry in range(2):
        rows = slice(128 * entry, 128 * (entry + 1))
        pick[rows, :] = dot00(stripe_hot, hits[entry].astype(BF16)).astype(BF16)
    small[2].wait()

    pl.semaphore_wait(barrier, 2 * CELLS - 1)

    def exchange(src, dst, rows, send, recv, view, first):
        def go(k):
            cell = lax.rem(my_c + k, CELLS)
            pltpu.make_async_remote_copy(
                src_ref=src.at[view * CELLS + cell, pl.ds(0, rows)],
                dst_ref=dst.at[me_slot, pl.ds(0, rows)],
                send_sem=send,
                recv_sem=recv,
                device_id=(cell, view),
                device_id_type=MESH,
            ).start()

        steps(first, CELLS, go)

    def settle(ref, count, rows, sem):
        part = ref.at[pl.ds(0, count), pl.ds(0, rows)]
        pltpu.make_async_copy(part, part, sem).wait()

    def own(src, dst):
        copy = pltpu.make_async_copy(src, dst, own_sem)
        copy.start()
        copy.wait()

    exchange(req, rreq, 1, req_send, req_recv, my_v, 1)
    exchange(req, rreq, 1, req_send, req_recv, 1 - my_v, 0)

    above = lax.rem(my_c + CELLS - 1, CELLS)
    below = lax.rem(my_c + 1, CELLS)

    def halo(buf, number, way):
        copy = pltpu.make_async_remote_copy(
            src_ref=buf.at[:, pl.ds(8 + 8 * way, 8), :],
            dst_ref=buf.at[:, pl.ds(24 - 24 * way, 8), :],
            send_sem=halo_send.at[2 * number + way],
            recv_sem=halo_recv.at[2 * number + way],
            device_id=(below if way else above, my_v),
            device_id_type=MESH,
        )
        copy.start()
        return copy

    target_halo = [halo(tpad, 0, way) for way in range(2)]
    own(req.at[me_slot], rreq.at[me_slot])
    settle(rreq, 255, 1, req_recv)

    asked = rreq[:, 0, :].astype(F32)
    turned = jnp.concatenate(
        [jnp.transpose(asked[0:128]), jnp.transpose(asked[128:256])], axis=1
    )
    want = turned[0:1, :].astype(jnp.int32)
    tile = turned[32:33, :].astype(jnp.int32)
    cols_in = jnp.where(my_v == 0, turned[64:65, 0:128], turned[64:65, 128:256]).astype(jnp.int32)
    t_stripe = quotient(tile, TILES)
    t_col = tile - TILES * t_stripe
    place = t_stripe - CELLS // 4
    place = jnp.where(place < 0, place + CELLS, place)
    side = (place >= CELLS // 2).astype(jnp.int32)
    anchor_x = (16 * t_col).astype(F32)
    anchor_y = (16 * (place - (CELLS // 2) * side)).astype(F32)
    view_d = (2 * (iota((1, 256), 1) // CELLS) + side).astype(F32)
    hot = (iota((NBP, 256), 0) == want).astype(F32)
    view_s[...] = jnp.broadcast_to(jnp.sum(hot * view_d, axis=1, keepdims=True), (NBP, 128))
    hot16 = hot.astype(BF16)

    pltpu.make_async_copy(par_s.at[:, pl.ds(0, NB), :], par_s.at[:, pl.ds(0, NB), :], load_sem.at[0]).wait()
    pltpu.make_async_copy(vis_s.at[:, pl.ds(0, NB), :], vis_s.at[:, pl.ds(0, NB), :], load_sem.at[1]).wait()

    def project(i, carry):
        rows = pl.ds(pl.multiple_of(8 * i, 8), 8)
        view = view_s[rows, :]
        seen = jnp.where(
            view < 1.5,
            jnp.where(view < 0.5, vis_s[0, rows, :], vis_s[1, rows, :]),
            jnp.where(view < 2.5, vis_s[2, rows, :], vis_s[3, rows, :]),
        )
        found = project_chunk(lambda f: par_s[f, rows, :], seen, cam, view)
        inside = iota((8, 128), 0) + 8 * i < NB
        for f in range(9):
            feat[f, rows, :] = jnp.where(inside, found[f], 0.0)
        return carry

    lax.fori_loop(0, NBP // 8, project, 0)

    live = want >= 0
    for f in range(9):
        high, mid, low = pieces(feat[f])
        got = (dot00(low, hot16) + dot00(mid, hot16)) + dot00(high, hot16)
        if f == 0:
            got = got - anchor_x
        if f == 1:
            got = got - anchor_y
        if f == 5:
            got = jnp.where(live, got, NEG)
        grid_f[0, f] = got[:, 0:128]
        grid_f[1, f] = got[:, 128:256]

    sub8 = iota((8, 128), 0).astype(F32)

    def render(view, part, sbuf):
        for quarter in (2 * part, 2 * part + 1):

            def blend(g, state):
                state = list(state)
                row = [
                    jnp.broadcast_to(grid_f[view, f, pl.ds(g, 1), :], (8, 128)) for f in range(9)
                ]
                dx = [sub8 - row[0], (sub8 + 8.0) - row[0]]
                lead = [row[2] * d * d + row[5] for d in dx]
                cross = [row[3] * d for d in dx]
                for line in range(4):
                    dy = (4.0 * quarter + line) - row[1]
                    bend = row[4] * dy
                    for half in range(2):
                        at = 4 * (2 * line + half)
                        alpha = jnp.exp2(lead[half] + dy * (cross[half] + bend))
                        weight = alpha * state[at + 3]
                        state[at] = state[at] + weight * row[6]
                        state[at + 1] = state[at + 1] + weight * row[7]
                        state[at + 2] = state[at + 2] + weight * row[8]
                        state[at + 3] = state[at + 3] - weight
                return tuple(state)

            zero = jnp.zeros((8, 128), F32)
            one = jnp.ones((8, 128), F32)
            state = lax.fori_loop(0, 128, blend, (zero, zero, zero, one) * 8, unroll=4)
            for at in range(8):
                start = 64 * (quarter % 2) + 8 * at
                for k in range(4):
                    px_s[k, start : start + 8, :] = state[4 * at + k]
        rows = pl.ds(pl.multiple_of(view * CELLS, CELLS), CELLS)
        for k in range(4):
            sbuf[rows, k, :] = jnp.transpose(px_s[k])

    sent = [sbuf0, sbuf1]
    got = [rbuf0, rbuf1]
    for part in range(2):
        render(my_v, part, sent[part])
        exchange(sent[part], got[part], 4, one_send.at[part], one_recv.at[part], my_v, 1)
        own(sent[part].at[me_slot], got[part].at[me_slot])
        render(1 - my_v, part, sent[part])
        exchange(sent[part], got[part], 4, one_send.at[part], one_recv.at[part], 1 - my_v, 0)

    taps = [0.0] * 6
    total = sum(2.718281828459045 ** (-(k * k) / 4.5) for k in range(-5, 6))
    for k in range(6):
        taps[k] = 2.718281828459045 ** (-(k * k) / 4.5) / total

    spot = lax.rem(my_c + CELLS - CELLS // 4, CELLS // 2)
    keep_top = jnp.where(spot != 0, 1.0, 0.0)
    keep_bottom = jnp.where(spot != CELLS // 2 - 1, 1.0, 0.0)

    def down_columns(terms):
        totals = [taps[0] * v for v in terms(0)]
        for k in range(1, 6):
            lower, upper = terms(-k), terms(k)
            totals = [t + taps[k] * (a + b) for t, a, b in zip(totals, lower, upper)]
        return totals

    def along_rows(count, out):
        def go(i, carry):
            plane = i // 2
            rows = pl.ds(pl.multiple_of(8 * (i % 2), 8), 8)
            x = vert[plane, rows, :]
            acc = taps[0] * x
            for k in range(1, 6):
                acc = acc + taps[k] * (pltpu.roll(x, k, 1) + pltpu.roll(x, 2048 - k, 1))
            out[plane, rows, :] = acc[:, 0:1920]
            return carry

        lax.fori_loop(0, 2 * count, go, 0)

    for copy in target_halo:
        copy.wait()
    tpad[:, 0:8, :] = tpad[:, 0:8, :] * keep_top
    tpad[:, 24:32, :] = tpad[:, 24:32, :] * keep_bottom
    for plane in range(9):
        vert[plane, :, 1920:2048] = jnp.zeros((16, 128), F32)

    def target_columns(j, carry):
        lanes = pl.ds(pl.multiple_of(128 * j, 128), 128)
        for ch in range(3):

            def terms(k):
                t = tpad[ch, 8 + k : 24 + k, lanes]
                return [t, t * t]

            found = down_columns(terms)
            vert[ch, :, lanes] = found[0]
            vert[3 + ch, :, lanes] = found[1]
        return carry

    lax.fori_loop(0, 15, target_columns, 0)
    along_rows(6, blur_t)

    settle(req, 255, 1, req_send)
    sent2 = [s2buf0, s2buf1]
    got2 = [r2buf0, r2buf1]

    for part in range(2):
        tiles, out, arrived = got[part], sent2[part], got2[part]
        settle(tiles, 255, 4, one_recv.at[part])

        hot = pick[...]
        pairs = []
        for k in (0, 2):
            parts = pieces(jnp.concatenate([tiles[:, k, :], tiles[:, k + 1, :]], axis=1))
            pairs.append((dot10(hot, parts[2]) + dot10(hot, parts[1])) + dot10(hot, parts[0]))
        clear = pairs[1][0:128, 128:256]
        for k in range(3):
            pair, lanes = pairs[k // 2], slice(128 * (k % 2), 128 * (k % 2) + 128)
            out[:, k, :] = pair[0:128, lanes] + clear * pair[128:256, lanes]

        def send_tile(k):
            cell = lax.rem(my_c + k, CELLS)
            pltpu.make_async_remote_copy(
                src_ref=out.at[cell, pl.ds(0, 3)],
                dst_ref=arrived.at[my_c, pl.ds(0, 3)],
                send_sem=two_send.at[part],
                recv_sem=two_recv.at[part],
                device_id=(cell, my_v),
                device_id_type=MESH,
            ).start()

        steps(1, CELLS, send_tile)
        own(out.at[my_c], arrived.at[my_c])
    settle(sbuf0, 255, 4, one_send.at[0])
    settle(sbuf1, 255, 4, one_send.at[1])

    hot_col = (iota((TILES, 128), 0) == cols_in).astype(BF16)
    sub_b = iota((15, 8, 128), 1)
    lane_b = iota((15, 8, 128), 2) // 16

    image_halo = []
    for part in range(2):
        settle(got2[part], 127, 3, two_recv.at[part])
        for ch in range(3):
            parts = pieces(got2[part][:, ch, :])
            found = (dot10(hot_col, parts[2]) + dot10(hot_col, parts[1])) + dot10(hot_col, parts[0])
            cube = found.reshape(15, 8, 128)
            for bit in (1, 2, 4):
                sub_bit = (sub_b & bit) != 0
                lane_bit = (lane_b & bit) != 0
                from_up = pltpu.roll(pltpu.roll(cube, bit, 1), 128 - 16 * bit, 2)
                from_down = pltpu.roll(pltpu.roll(cube, 8 - bit, 1), 16 * bit, 2)
                cube = jnp.where(sub_bit == lane_bit, cube, jnp.where(sub_bit, from_up, from_down))
            for j in range(15):
                ipad[ch, 8 + 8 * part : 16 + 8 * part, 128 * j : 128 * (j + 1)] = cube[j]
        image_halo.append(halo(ipad, 1, part))

    image_out[...] = ipad[:, 8:24, :]
    for part in range(2):
        settle(sent2[part], 127, 3, two_send.at[part])
    for copy in image_halo:
        copy.wait()
    ipad[:, 0:8, :] = ipad[:, 0:8, :] * keep_top
    ipad[:, 24:32, :] = ipad[:, 24:32, :] * keep_bottom

    def image_columns(j, carry):
        lanes = pl.ds(pl.multiple_of(128 * j, 128), 128)
        for ch in range(3):

            def terms(k):
                x = ipad[ch, 8 + k : 24 + k, lanes]
                return [x, x * x, x * tpad[ch, 8 + k : 24 + k, lanes]]

            found = down_columns(terms)
            for n in range(3):
                vert[3 * n + ch, :, lanes] = found[n]
        return carry

    lax.fori_loop(0, 15, image_columns, 0)
    along_rows(9, blur_i)

    def finish(j, carry):
        lanes = pl.ds(pl.multiple_of(128 * j, 128), 128)
        apart = jnp.zeros((16, 128), F32)
        alike = jnp.zeros((16, 128), F32)
        for ch in range(3):
            mx, sxx, sxy = [blur_i[3 * n + ch, :, lanes] for n in range(3)]
            my, syy = blur_t[ch, :, lanes], blur_t[3 + ch, :, lanes]
            mxx, myy, mxy = mx * mx, my * my, mx * my
            above_line = (2.0 * mxy + 0.0001) * (2.0 * (sxy - mxy) + 0.0009)
            below_line = (mxx + myy + 0.0001) * ((sxx - mxx) + (syy - myy) + 0.0009)
            alike = alike + above_line / below_line
            apart = apart + jnp.abs(ipad[ch, 8:24, lanes] - tpad[ch, 8:24, lanes])
        loss_out[:, lanes] = 0.8 * (apart * (1.0 / 3.0)) + 0.2 * (1.0 - alike * (1.0 / 3.0))
        return carry

    lax.fori_loop(0, 15, finish, 0)


def local(gauss_params, visible, cameras, tile_ids, tile_blocks, target):
    vmem = pl.BlockSpec(memory_space=pltpu.VMEM)
    hbm = pl.BlockSpec(memory_space=pltpu.HBM)
    dma = pltpu.SemaphoreType.DMA
    image, loss = pl.pallas_call(
        kernel,
        out_shape=(
            jax.ShapeDtypeStruct((3, 16, 1920), F32),
            jax.ShapeDtypeStruct((16, 1920), F32),
        ),
        in_specs=[hbm, hbm, pl.BlockSpec(memory_space=pltpu.SMEM), hbm, hbm, hbm],
        out_specs=(vmem, vmem),
        scratch_shapes=[
            pltpu.VMEM((59, NBP, 128), F32),
            pltpu.VMEM((4, NBP, 128), jnp.int32),
            pltpu.VMEM((1, TILES), jnp.int32),
            pltpu.VMEM((2, TILES), jnp.int32),
            pltpu.VMEM((8, 128), F32),
            pltpu.VMEM((256, 256), BF16),
            pltpu.VMEM((256, 1, 128), jnp.int32),
            pltpu.VMEM((256, 1, 128), jnp.int32),
            pltpu.VMEM((NBP, 128), F32),
            pltpu.VMEM((9, NBP, 128), F32),
            pltpu.VMEM((2, 9, 128, 128), F32),
            pltpu.VMEM((4, 128, 128), F32),
            pltpu.VMEM((256, 4, 128), F32),
            pltpu.VMEM((256, 4, 128), F32),
            pltpu.VMEM((256, 4, 128), F32),
            pltpu.VMEM((256, 4, 128), F32),
            pltpu.VMEM((128, 4, 128), F32),
            pltpu.VMEM((128, 4, 128), F32),
            pltpu.VMEM((128, 4, 128), F32),
            pltpu.VMEM((128, 4, 128), F32),
            pltpu.VMEM((3, 32, 1920), F32),
            pltpu.VMEM((3, 32, 1920), F32),
            pltpu.VMEM((9, 16, 2048), F32),
            pltpu.VMEM((6, 16, 1920), F32),
            pltpu.VMEM((9, 16, 1920), F32),
            dma((2,)),
            dma((4,)),
            dma,
            dma,
            dma((4,)),
            dma((4,)),
            dma((2,)),
            dma((2,)),
            dma((2,)),
            dma((2,)),
            dma,
        ],
        compiler_params=pltpu.CompilerParams(
            collective_id=0, has_side_effects=True, vmem_limit_bytes=60 << 20
        ),
    )(gauss_params, visible, cameras, tile_ids[0], tile_blocks[0, 0].T, target[0])
    return (image[None], loss[None])


def solution(mesh):
    return jax.shard_map(
        local,
        mesh=mesh,
        in_specs=(
            P(None, ("cell", "view")),
            P(None, ("cell", "view")),
            P(),
            P("cell", "view", None),
            P("cell", "view", None, None),
            P("view", None, "cell", None),
        ),
        out_specs=(P("view", None, "cell", None), P("view", "cell", None)),
        check_vma=False,
    )
```

```python
import functools

import jax
import jax.numpy as jnp
from jax import lax
from jax.experimental import pallas as pl
from jax.experimental.pallas import tpu as pltpu
from jax.sharding import PartitionSpec as P

MESH = pl.DeviceIdType.MESH
F32 = jnp.float32
BF16 = jnp.bfloat16
LOG2E = 1.4426950408889634
NEG = -1e30
NB = 150
NBP = 152
CELLS = 128
TILES = 120


def dot00(left, right):
    return lax.dot_general(left, right, (((0,), (0,)), ((), ())), preferred_element_type=F32)


def dot10(left, right):
    return lax.dot_general(left, right, (((1,), (0,)), ((), ())), preferred_element_type=F32)


def pieces(value):
    high = value.astype(BF16)
    rest = value - high.astype(F32)
    mid = rest.astype(BF16)
    low = (rest - mid.astype(F32)).astype(BF16)
    return high, mid, low


def iota(shape, dim):
    return lax.broadcasted_iota(jnp.int32, shape, dim)


def quotient(value, divisor):
    return ((value.astype(F32) + 0.5) * (1.0 / divisor)).astype(jnp.int32)


def harmonics(ux, uy, uz):
    xx, yy, zz = ux * ux, uy * uy, uz * uz
    return [
        None,
        -0.4886025119029199 * uy,
        0.4886025119029199 * uz,
        -0.4886025119029199 * ux,
        1.0925484305920792 * ux * uy,
        -1.0925484305920792 * uy * uz,
        0.31539156525252005 * (2.0 * zz - xx - yy),
        -1.0925484305920792 * ux * uz,
        0.5462742152960396 * (xx - yy),
        -0.5900435899266435 * uy * (3.0 * xx - yy),
        2.890611442640554 * ux * uy * uz,
        -0.4570457994644658 * uy * (4.0 * zz - xx - yy),
        0.3731763325901154 * uz * (2.0 * zz - 3.0 * xx - 3.0 * yy),
        -0.4570457994644658 * ux * (4.0 * zz - xx - yy),
        1.445305721320277 * uz * (xx - yy),
        -0.5900435899266435 * ux * (xx - 3.0 * yy),
    ]


def project_chunk(raw, seen, cam, view):
    def pick(entry):
        return jnp.where(
            view < 1.5,
            jnp.where(view < 0.5, cam[0, entry], cam[1, entry]),
            jnp.where(view < 2.5, cam[2, entry], cam[3, entry]),
        )

    e = [pick(entry) for entry in range(15)]
    rot = [e[0:3], e[3:6], e[6:9]]
    off = e[9:12]
    focal = e[12]
    pos = [raw(n) for n in range(3)]
    pc = [rot[m][0] * pos[0] + rot[m][1] * pos[1] + rot[m][2] * pos[2] + off[m] for m in range(3)]
    inv_z = 1.0 / pc[2]
    fz = focal * inv_z
    sx = focal * pc[0] / pc[2] + e[13]
    sy = focal * pc[1] / pc[2] + e[14]
    q = [raw(6 + n) for n in range(4)]
    scale = 1.0 / jnp.sqrt(q[0] * q[0] + q[1] * q[1] + q[2] * q[2] + q[3] * q[3])
    r, x, y, z = [part * scale for part in q]
    turn = [
        [1.0 - 2.0 * (y * y + z * z), 2.0 * (x * y - r * z), 2.0 * (x * z + r * y)],
        [2.0 * (x * y + r * z), 1.0 - 2.0 * (x * x + z * z), 2.0 * (y * z - r * x)],
        [2.0 * (x * z - r * y), 2.0 * (y * z + r * x), 1.0 - 2.0 * (x * x + y * y)],
    ]
    sq = [jnp.exp(2.0 * raw(3 + n)) for n in range(3)]
    jz = [-fz * pc[0] * inv_z, -fz * pc[1] * inv_z]
    cams = [[fz * rot[m][k] + jz[m] * rot[2][k] for k in range(3)] for m in range(2)]
    w = [
        [cams[m][0] * turn[0][k] + cams[m][1] * turn[1][k] + cams[m][2] * turn[2][k] for k in range(3)]
        for m in range(2)
    ]
    s0 = [sq[k] * w[0][k] for k in range(3)]
    cov_a = s0[0] * w[0][0] + s0[1] * w[0][1] + s0[2] * w[0][2] + 0.3
    cov_b = s0[0] * w[1][0] + s0[1] * w[1][1] + s0[2] * w[1][2]
    cov_c = sq[0] * w[1][0] * w[1][0] + sq[1] * w[1][1] * w[1][1] + sq[2] * w[1][2] * w[1][2] + 0.3
    inv_det = 1.0 / (cov_a * cov_c - cov_b * cov_b)
    eye = [-(rot[0][k] * off[0] + rot[1][k] * off[1] + rot[2][k] * off[2]) for k in range(3)]
    head = [pos[k] - eye[k] for k in range(3)]
    inv_len = 1.0 / jnp.sqrt(head[0] * head[0] + head[1] * head[1] + head[2] * head[2])
    basis = harmonics(head[0] * inv_len, head[1] * inv_len, head[2] * inv_len)
    colours = []
    for k in range(3):
        total = 0.5 + 0.28209479177387814 * raw(11 + k)
        for j in range(1, 16):
            total = total + basis[j] * raw(11 + 3 * j + k)
        colours.append(jnp.maximum(total, 0.0))
    log_o = jnp.maximum(-LOG2E * jnp.log1p(jnp.exp(-raw(10))), NEG)
    log_o = jnp.where(seen > 0, log_o, NEG)
    return [
        sx,
        sy,
        (-0.5 * LOG2E) * (cov_c * inv_det),
        LOG2E * (cov_b * inv_det),
        (-0.5 * LOG2E) * (cov_a * inv_det),
        log_o,
    ] + colours


def steps(first, last, body):
    def eight(i, carry):
        for n in range(8):
            body(first + 8 * i + n)
        return carry

    whole = (last - first) // 8
    lax.fori_loop(0, whole, eight, 0)
    for k in range(first + 8 * whole, last):
        body(k)


def kernel(
    params,
    visible,
    cam,
    tile_ids,
    tile_blocks,
    target,
    image_out,
    loss_out,
    par_s,
    vis_s,
    tid_i,
    blk_i,
    list_s,
    pick,
    req,
    rreq,
    view_s,
    feat,
    grid_f,
    px_s,
    sbuf0,
    sbuf1,
    rbuf0,
    rbuf1,
    s2buf0,
    s2buf1,
    r2buf0,
    r2buf1,
    tpad,
    ipad,
    edge_out,
    edge_in,
    vert,
    blur_t,
    blur_i,
    load_sem,
    small_sem,
    req_send,
    req_recv,
    halo_send,
    halo_recv,
    one_send,
    one_recv,
    two_send,
    two_recv,
    own_sem,
):
    my_c = lax.axis_index("cell")
    my_v = lax.axis_index("view")
    me_slot = my_v * CELLS + my_c

    barrier = pltpu.get_barrier_semaphore()

    small = [
        pltpu.make_async_copy(tile_ids, tid_i, small_sem.at[0]),
        pltpu.make_async_copy(tile_blocks, blk_i, small_sem.at[1]),
        pltpu.make_async_copy(target, tpad.at[:, pl.ds(8, 16), :], small_sem.at[2]),
    ]
    for copy in small:
        copy.start()

    def greet(k):
        cell = (my_c + k) & (CELLS - 1)
        pl.semaphore_signal(barrier, inc=1, device_id=(cell, my_v), device_id_type=MESH)
        pl.semaphore_signal(barrier, inc=1, device_id=(cell, 1 - my_v), device_id_type=MESH)

    pl.semaphore_signal(barrier, inc=1, device_id=(my_c, 1 - my_v), device_id_type=MESH)
    steps(1, CELLS, greet)

    par_s[:, NB:NBP, :] = jnp.zeros((59, NBP - NB, 128), F32)
    vis_s[:, NB:NBP, :] = jnp.zeros((4, NBP - NB, 128), jnp.int32)

    def load(b, carry):
        lanes = pl.ds(pl.multiple_of(b * 128, 128), 128)
        pltpu.make_async_copy(params.at[:, lanes], par_s.at[:, b, :], load_sem.at[0]).start()
        pltpu.make_async_copy(visible.at[:, lanes], vis_s.at[:, b, :], load_sem.at[1]).start()
        return carry

    lax.fori_loop(0, NB, load, 0)

    list_s[...] = jnp.full((8, 128), -1.0, F32)
    small[0].wait()
    small[1].wait()
    list_s[0:1, 0:TILES] = tid_i[...].astype(F32)
    list_s[1:3, 0:TILES] = blk_i[...].astype(F32)
    lists = jnp.transpose(list_s[...])[0:TILES].astype(jnp.int32)
    tid = lists[:, 0:1]
    stripe = quotient(tid, TILES)
    column = tid - TILES * stripe
    lane2 = iota((TILES, 256), 1)
    hits = []
    local = []
    for entry in range(2):
        block = lists[:, 1 + entry : 2 + entry]
        owner = quotient(jnp.maximum(block, 0), NB)
        cell = owner // 2
        slot = (owner - 2 * cell) * CELLS + cell
        slot = jnp.where(block >= 0, slot, -1)
        hits.append((slot == lane2).astype(F32))
        local.append((block - NB * owner + 1).astype(F32))
    by_stripe = (stripe == iota((TILES, 128), 1)).astype(F32)
    lb_row = jnp.sum(hits[0] * local[0] + hits[1] * local[1], axis=0, keepdims=True) - 1.0
    tl_row = jnp.sum((hits[0] + hits[1]) * tid.astype(F32), axis=0, keepdims=True)
    col_row = jnp.sum(by_stripe * (column + 1).astype(F32), axis=0, keepdims=True) - 1.0
    sub = iota((128, 128), 0)
    for part in range(2):
        lanes = slice(128 * part, 128 * (part + 1))
        text = jnp.where(
            sub < 32, lb_row[:, lanes], jnp.where(sub < 64, tl_row[:, lanes], col_row)
        )
        req[lanes, 0, :] = jnp.transpose(text).astype(jnp.int32)
    stripe_hot = by_stripe.astype(BF16)
    for entry in range(2):
        rows = slice(128 * entry, 128 * (entry + 1))
        pick[rows, :] = dot00(stripe_hot, hits[entry].astype(BF16)).astype(BF16)
    small[2].wait()

    pl.semaphore_wait(barrier, 2 * CELLS - 1)

    def exchange(src, dst, rows, send, recv, view, first):
        def go(k):
            cell = (my_c + k) & (CELLS - 1)
            pltpu.make_async_remote_copy(
                src_ref=src.at[view * CELLS + cell, pl.ds(0, rows)],
                dst_ref=dst.at[me_slot, pl.ds(0, rows)],
                send_sem=send,
                recv_sem=recv,
                device_id=(cell, view),
                device_id_type=MESH,
            ).start()

        steps(first, CELLS, go)

    def settle(ref, count, rows, sem):
        part = ref.at[pl.ds(0, count), pl.ds(0, rows)]
        pltpu.make_async_copy(part, part, sem).wait()

    def own(src, dst):
        copy = pltpu.make_async_copy(src, dst, own_sem)
        copy.start()
        copy.wait()

    exchange(req, rreq, 1, req_send, req_recv, my_v, 1)
    exchange(req, rreq, 1, req_send, req_recv, 1 - my_v, 0)

    above = lax.rem(my_c + CELLS - 1, CELLS)
    below = lax.rem(my_c + 1, CELLS)

    def halo(buf, number, way):
        if way:
            edge_out[number, :, 0:5, :] = buf[:, 19:24, :]
            src, dst = edge_out.at[number, :, pl.ds(0, 5), :], edge_in.at[number, :, pl.ds(0, 5), :]
        else:
            src, dst = buf.at[:, pl.ds(8, 5), :], buf.at[:, pl.ds(24, 5), :]
        copy = pltpu.make_async_remote_copy(
            src_ref=src,
            dst_ref=dst,
            send_sem=halo_send.at[2 * number + way],
            recv_sem=halo_recv.at[2 * number + way],
            device_id=(below if way else above, my_v),
            device_id_type=MESH,
        )
        copy.start()
        return copy

    target_halo = [halo(tpad, 0, way) for way in range(2)]
    own(req.at[me_slot], rreq.at[me_slot])
    settle(rreq, 255, 1, req_recv)

    asked = rreq[:, 0, :].astype(F32)
    turned = jnp.concatenate(
        [jnp.transpose(asked[0:128]), jnp.transpose(asked[128:256])], axis=1
    )
    want = turned[0:1, :].astype(jnp.int32)
    tile = turned[32:33, :].astype(jnp.int32)
    cols_in = jnp.where(my_v == 0, turned[64:65, 0:128], turned[64:65, 128:256]).astype(jnp.int32)
    t_stripe = quotient(tile, TILES)
    t_col = tile - TILES * t_stripe
    place = t_stripe - CELLS // 4
    place = jnp.where(place < 0, place + CELLS, place)
    side = (place >= CELLS // 2).astype(jnp.int32)
    anchor_x = (16 * t_col).astype(F32)
    anchor_y = (16 * (place - (CELLS // 2) * side)).astype(F32)
    view_d = (2 * (iota((1, 256), 1) // CELLS) + side).astype(F32)
    hot = (iota((NBP, 256), 0) == want).astype(F32)
    view_s[...] = jnp.broadcast_to(jnp.sum(hot * view_d, axis=1, keepdims=True), (NBP, 128))
    hot16 = hot.astype(BF16)

    pltpu.make_async_copy(par_s.at[:, pl.ds(0, NB), :], par_s.at[:, pl.ds(0, NB), :], load_sem.at[0]).wait()
    pltpu.make_async_copy(vis_s.at[:, pl.ds(0, NB), :], vis_s.at[:, pl.ds(0, NB), :], load_sem.at[1]).wait()

    def project(i, carry):
        rows = pl.ds(pl.multiple_of(8 * i, 8), 8)
        view = view_s[rows, :]
        seen = jnp.where(
            view < 1.5,
            jnp.where(view < 0.5, vis_s[0, rows, :], vis_s[1, rows, :]),
            jnp.where(view < 2.5, vis_s[2, rows, :], vis_s[3, rows, :]),
        )
        found = project_chunk(lambda f: par_s[f, rows, :], seen, cam, view)
        inside = iota((8, 128), 0) + 8 * i < NB
        for f in range(9):
            feat[f, rows, :] = jnp.where(inside, found[f], 0.0)
        return carry

    lax.fori_loop(0, NBP // 8, project, 0)

    live = want >= 0
    for f in range(9):
        high, mid, low = pieces(feat[f])
        got = (dot00(low, hot16) + dot00(mid, hot16)) + dot00(high, hot16)
        if f == 0:
            got = got - anchor_x
        if f == 1:
            got = got - anchor_y
        if f == 5:
            got = jnp.where(live, got, NEG)
        grid_f[0, f] = got[:, 0:128]
        grid_f[1, f] = got[:, 128:256]

    sub8 = iota((8, 128), 0).astype(F32)

    def render(view, part, sbuf):
        for quarter in (2 * part, 2 * part + 1):

            def blend(g, state):
                state = list(state)
                row = [
                    jnp.broadcast_to(grid_f[view, f, pl.ds(g, 1), :], (8, 128)) for f in range(9)
                ]
                dx = [sub8 - row[0], (sub8 + 8.0) - row[0]]
                lead = [row[2] * d * d + row[5] for d in dx]
                cross = [row[3] * d for d in dx]
                for line in range(4):
                    dy = (4.0 * quarter + line) - row[1]
                    bend = row[4] * dy
                    for half in range(2):
                        at = 4 * (2 * line + half)
                        alpha = jnp.exp2(lead[half] + dy * (cross[half] + bend))
                        weight = alpha * state[at + 3]
                        state[at] = state[at] + weight * row[6]
                        state[at + 1] = state[at + 1] + weight * row[7]
                        state[at + 2] = state[at + 2] + weight * row[8]
                        state[at + 3] = state[at + 3] - weight
                return tuple(state)

            zero = jnp.zeros((8, 128), F32)
            one = jnp.ones((8, 128), F32)
            state = lax.fori_loop(0, 128, blend, (zero, zero, zero, one) * 8, unroll=4)
            for at in range(8):
                start = 64 * (quarter % 2) + 8 * at
                for k in range(4):
                    px_s[k, start : start + 8, :] = state[4 * at + k]
        rows = pl.ds(pl.multiple_of(view * CELLS, CELLS), CELLS)
        for k in range(4):
            sbuf[rows, k, :] = jnp.transpose(px_s[k])

    sent = [sbuf0, sbuf1]
    got = [rbuf0, rbuf1]
    for part in range(2):
        render(my_v, part, sent[part])
        exchange(sent[part], got[part], 4, one_send.at[part], one_recv.at[part], my_v, 1)
        own(sent[part].at[me_slot], got[part].at[me_slot])
        render(1 - my_v, part, sent[part])
        exchange(sent[part], got[part], 4, one_send.at[part], one_recv.at[part], 1 - my_v, 0)

    taps = [0.0] * 6
    total = sum(2.718281828459045 ** (-(k * k) / 4.5) for k in range(-5, 6))
    for k in range(6):
        taps[k] = 2.718281828459045 ** (-(k * k) / 4.5) / total

    spot = lax.rem(my_c + CELLS - CELLS // 4, CELLS // 2)
    keep_top = jnp.where(spot != 0, 1.0, 0.0)
    keep_bottom = jnp.where(spot != CELLS // 2 - 1, 1.0, 0.0)

    def down_columns(terms):
        totals = [taps[0] * v for v in terms(0)]
        for k in range(1, 6):
            lower, upper = terms(-k), terms(k)
            totals = [t + taps[k] * (a + b) for t, a, b in zip(totals, lower, upper)]
        return totals

    def along_rows(count, out):
        def go(i, carry):
            plane = i // 2
            rows = pl.ds(pl.multiple_of(8 * (i % 2), 8), 8)
            x = vert[plane, rows, :]
            acc = taps[0] * x
            for k in range(1, 6):
                acc = acc + taps[k] * (pltpu.roll(x, k, 1) + pltpu.roll(x, 2048 - k, 1))
            out[plane, rows, :] = acc[:, 0:1920]
            return carry

        lax.fori_loop(0, 2 * count, go, 0, unroll=6)

    for copy in target_halo:
        copy.wait()
    tpad[:, 3:8, :] = edge_in[0, :, 0:5, :] * keep_top
    tpad[:, 24:29, :] = tpad[:, 24:29, :] * keep_bottom
    for plane in range(9):
        vert[plane, :, 1920:2048] = jnp.zeros((16, 128), F32)

    def target_columns(j, carry):
        lanes = pl.ds(pl.multiple_of(128 * j, 128), 128)
        for ch in range(3):

            def terms(k):
                t = tpad[ch, 8 + k : 24 + k, lanes]
                return [t, t * t]

            found = down_columns(terms)
            vert[ch, :, lanes] = found[0]
            vert[3 + ch, :, lanes] = found[1]
        return carry

    lax.fori_loop(0, 15, target_columns, 0)
    along_rows(6, blur_t)

    settle(req, 255, 1, req_send)
    sent2 = [s2buf0, s2buf1]
    got2 = [r2buf0, r2buf1]

    for part in range(2):
        tiles, out, arrived = got[part], sent2[part], got2[part]
        settle(tiles, 255, 4, one_recv.at[part])

        hot = pick[...]
        pairs = []
        for k in (0, 2):
            parts = pieces(jnp.concatenate([tiles[:, k, :], tiles[:, k + 1, :]], axis=1))
            pairs.append((dot10(hot, parts[2]) + dot10(hot, parts[1])) + dot10(hot, parts[0]))
        clear = pairs[1][0:128, 128:256]
        for k in range(3):
            pair, lanes = pairs[k // 2], slice(128 * (k % 2), 128 * (k % 2) + 128)
            out[:, k, :] = pair[0:128, lanes] + clear * pair[128:256, lanes]

        def send_tile(k):
            cell = (my_c + k) & (CELLS - 1)
            pltpu.make_async_remote_copy(
                src_ref=out.at[cell, pl.ds(0, 3)],
                dst_ref=arrived.at[my_c, pl.ds(0, 3)],
                send_sem=two_send.at[part],
                recv_sem=two_recv.at[part],
                device_id=(cell, my_v),
                device_id_type=MESH,
            ).start()

        steps(1, CELLS, send_tile)
        own(out.at[my_c], arrived.at[my_c])
    settle(sbuf0, 255, 4, one_send.at[0])
    settle(sbuf1, 255, 4, one_send.at[1])

    hot_col = (iota((TILES, 128), 0) == cols_in).astype(BF16)
    sub_b = iota((15, 8, 128), 1)
    lane_b = iota((15, 8, 128), 2) // 16

    image_halo = []
    for part in range(2):
        settle(got2[part], 127, 3, two_recv.at[part])
        for ch in range(3):
            parts = pieces(got2[part][:, ch, :])
            found = (dot10(hot_col, parts[2]) + dot10(hot_col, parts[1])) + dot10(hot_col, parts[0])
            cube = found.reshape(15, 8, 128)
            for bit in (1, 2, 4):
                sub_bit = (sub_b & bit) != 0
                lane_bit = (lane_b & bit) != 0
                from_up = pltpu.roll(pltpu.roll(cube, bit, 1), 128 - 16 * bit, 2)
                from_down = pltpu.roll(pltpu.roll(cube, 8 - bit, 1), 16 * bit, 2)
                cube = jnp.where(sub_bit == lane_bit, cube, jnp.where(sub_bit, from_up, from_down))
            for j in range(15):
                ipad[ch, 8 + 8 * part : 16 + 8 * part, 128 * j : 128 * (j + 1)] = cube[j]
        image_halo.append(halo(ipad, 1, part))

    image_copy = pltpu.make_async_copy(ipad.at[:, pl.ds(8, 16), :], image_out, small_sem.at[3])
    image_copy.start()
    for part in range(2):
        settle(sent2[part], 127, 3, two_send.at[part])
    for copy in image_halo:
        copy.wait()
    ipad[:, 3:8, :] = edge_in[1, :, 0:5, :] * keep_top
    ipad[:, 24:29, :] = ipad[:, 24:29, :] * keep_bottom

    def image_columns(j, carry):
        lanes = pl.ds(pl.multiple_of(128 * j, 128), 128)
        for ch in range(3):

            def terms(k):
                x = ipad[ch, 8 + k : 24 + k, lanes]
                return [x, x * x, x * tpad[ch, 8 + k : 24 + k, lanes]]

            found = down_columns(terms)
            for n in range(3):
                vert[3 * n + ch, :, lanes] = found[n]
        return carry

    lax.fori_loop(0, 15, image_columns, 0)
    along_rows(9, blur_i)

    def finish(j, carry):
        lanes = pl.ds(pl.multiple_of(128 * j, 128), 128)
        apart = jnp.zeros((16, 128), F32)
        alike = jnp.zeros((16, 128), F32)
        for ch in range(3):
            mx, sxx, sxy = [blur_i[3 * n + ch, :, lanes] for n in range(3)]
            my, syy = blur_t[ch, :, lanes], blur_t[3 + ch, :, lanes]
            mxx, myy, mxy = mx * mx, my * my, mx * my
            above_line = (2.0 * mxy + 0.0001) * (2.0 * (sxy - mxy) + 0.0009)
            below_line = (mxx + myy + 0.0001) * ((sxx - mxx) + (syy - myy) + 0.0009)
            alike = alike + above_line / below_line
            apart = apart + jnp.abs(ipad[ch, 8:24, lanes] - tpad[ch, 8:24, lanes])
        loss_out[:, lanes] = 0.8 * (apart * (1.0 / 3.0)) + 0.2 * (1.0 - alike * (1.0 / 3.0))
        return carry

    lax.fori_loop(0, 15, finish, 0)
    image_copy.wait()


def local(gauss_params, visible, cameras, tile_ids, tile_blocks, target):
    vmem = pl.BlockSpec(memory_space=pltpu.VMEM)
    hbm = pl.BlockSpec(memory_space=pltpu.HBM)
    dma = pltpu.SemaphoreType.DMA
    image, loss = pl.pallas_call(
        kernel,
        out_shape=(
            jax.ShapeDtypeStruct((3, 16, 1920), F32),
            jax.ShapeDtypeStruct((16, 1920), F32),
        ),
        in_specs=[hbm, hbm, pl.BlockSpec(memory_space=pltpu.SMEM), hbm, hbm, hbm],
        out_specs=(hbm, vmem),
        scratch_shapes=[
            pltpu.VMEM((59, NBP, 128), F32),
            pltpu.VMEM((4, NBP, 128), jnp.int32),
            pltpu.VMEM((1, TILES), jnp.int32),
            pltpu.VMEM((2, TILES), jnp.int32),
            pltpu.VMEM((8, 128), F32),
            pltpu.VMEM((256, 256), BF16),
            pltpu.VMEM((256, 1, 128), jnp.int32),
            pltpu.VMEM((256, 1, 128), jnp.int32),
            pltpu.VMEM((NBP, 128), F32),
            pltpu.VMEM((9, NBP, 128), F32),
            pltpu.VMEM((2, 9, 128, 128), F32),
            pltpu.VMEM((4, 128, 128), F32),
            pltpu.VMEM((256, 4, 128), F32),
            pltpu.VMEM((256, 4, 128), F32),
            pltpu.VMEM((256, 4, 128), F32),
            pltpu.VMEM((256, 4, 128), F32),
            pltpu.VMEM((128, 4, 128), F32),
            pltpu.VMEM((128, 4, 128), F32),
            pltpu.VMEM((128, 4, 128), F32),
            pltpu.VMEM((128, 4, 128), F32),
            pltpu.VMEM((3, 32, 1920), F32),
            pltpu.VMEM((3, 32, 1920), F32),
            pltpu.VMEM((2, 3, 8, 1920), F32),
            pltpu.VMEM((2, 3, 8, 1920), F32),
            pltpu.VMEM((9, 16, 2048), F32),
            pltpu.VMEM((6, 16, 1920), F32),
            pltpu.VMEM((9, 16, 1920), F32),
            dma((2,)),
            dma((4,)),
            dma,
            dma,
            dma((4,)),
            dma((4,)),
            dma((2,)),
            dma((2,)),
            dma((2,)),
            dma((2,)),
            dma,
        ],
        compiler_params=pltpu.CompilerParams(
            collective_id=0, has_side_effects=True, vmem_limit_bytes=60 << 20
        ),
    )(gauss_params, visible, cameras, tile_ids[0], tile_blocks[0, 0].T, target[0])
    return (image[None], loss[None])


def solution(mesh):
    return jax.shard_map(
        local,
        mesh=mesh,
        in_specs=(
            P(None, ("cell", "view")),
            P(None, ("cell", "view")),
            P(),
            P("cell", "view", None),
            P("cell", "view", None, None),
            P("view", None, "cell", None),
        ),
        out_specs=(P("view", None, "cell", None), P("view", "cell", None)),
        check_vma=False,
    )
```

```python
import functools

import jax
import jax.numpy as jnp
from jax import lax
from jax.experimental import pallas as pl
from jax.experimental.pallas import tpu as pltpu
from jax.sharding import PartitionSpec as P

MESH = pl.DeviceIdType.MESH
F32 = jnp.float32
BF16 = jnp.bfloat16
LOG2E = 1.4426950408889634
NEG = -1e30
NB = 150
NBP = 152
CELLS = 128
TILES = 120


def dot00(left, right):
    return lax.dot_general(left, right, (((0,), (0,)), ((), ())), preferred_element_type=F32)


def dot10(left, right):
    return lax.dot_general(left, right, (((1,), (0,)), ((), ())), preferred_element_type=F32)


def pieces(value):
    high = value.astype(BF16)
    rest = value - high.astype(F32)
    mid = rest.astype(BF16)
    low = (rest - mid.astype(F32)).astype(BF16)
    return high, mid, low


def iota(shape, dim):
    return lax.broadcasted_iota(jnp.int32, shape, dim)


def quotient(value, divisor):
    return ((value.astype(F32) + 0.5) * (1.0 / divisor)).astype(jnp.int32)


def harmonics(ux, uy, uz):
    xx, yy, zz = ux * ux, uy * uy, uz * uz
    return [
        None,
        -0.4886025119029199 * uy,
        0.4886025119029199 * uz,
        -0.4886025119029199 * ux,
        1.0925484305920792 * ux * uy,
        -1.0925484305920792 * uy * uz,
        0.31539156525252005 * (2.0 * zz - xx - yy),
        -1.0925484305920792 * ux * uz,
        0.5462742152960396 * (xx - yy),
        -0.5900435899266435 * uy * (3.0 * xx - yy),
        2.890611442640554 * ux * uy * uz,
        -0.4570457994644658 * uy * (4.0 * zz - xx - yy),
        0.3731763325901154 * uz * (2.0 * zz - 3.0 * xx - 3.0 * yy),
        -0.4570457994644658 * ux * (4.0 * zz - xx - yy),
        1.445305721320277 * uz * (xx - yy),
        -0.5900435899266435 * ux * (xx - 3.0 * yy),
    ]


def project_chunk(raw, seen, cam, view):
    def pick(entry):
        return jnp.where(
            view < 1.5,
            jnp.where(view < 0.5, cam[0, entry], cam[1, entry]),
            jnp.where(view < 2.5, cam[2, entry], cam[3, entry]),
        )

    e = [pick(entry) for entry in range(15)]
    rot = [e[0:3], e[3:6], e[6:9]]
    off = e[9:12]
    focal = e[12]
    pos = [raw(n) for n in range(3)]
    pc = [rot[m][0] * pos[0] + rot[m][1] * pos[1] + rot[m][2] * pos[2] + off[m] for m in range(3)]
    inv_z = 1.0 / pc[2]
    fz = focal * inv_z
    sx = focal * pc[0] / pc[2] + e[13]
    sy = focal * pc[1] / pc[2] + e[14]
    q = [raw(6 + n) for n in range(4)]
    scale = 1.0 / jnp.sqrt(q[0] * q[0] + q[1] * q[1] + q[2] * q[2] + q[3] * q[3])
    r, x, y, z = [part * scale for part in q]
    turn = [
        [1.0 - 2.0 * (y * y + z * z), 2.0 * (x * y - r * z), 2.0 * (x * z + r * y)],
        [2.0 * (x * y + r * z), 1.0 - 2.0 * (x * x + z * z), 2.0 * (y * z - r * x)],
        [2.0 * (x * z - r * y), 2.0 * (y * z + r * x), 1.0 - 2.0 * (x * x + y * y)],
    ]
    sq = [jnp.exp(2.0 * raw(3 + n)) for n in range(3)]
    jz = [-fz * pc[0] * inv_z, -fz * pc[1] * inv_z]
    cams = [[fz * rot[m][k] + jz[m] * rot[2][k] for k in range(3)] for m in range(2)]
    w = [
        [cams[m][0] * turn[0][k] + cams[m][1] * turn[1][k] + cams[m][2] * turn[2][k] for k in range(3)]
        for m in range(2)
    ]
    s0 = [sq[k] * w[0][k] for k in range(3)]
    cov_a = s0[0] * w[0][0] + s0[1] * w[0][1] + s0[2] * w[0][2] + 0.3
    cov_b = s0[0] * w[1][0] + s0[1] * w[1][1] + s0[2] * w[1][2]
    cov_c = sq[0] * w[1][0] * w[1][0] + sq[1] * w[1][1] * w[1][1] + sq[2] * w[1][2] * w[1][2] + 0.3
    inv_det = 1.0 / (cov_a * cov_c - cov_b * cov_b)
    eye = [-(rot[0][k] * off[0] + rot[1][k] * off[1] + rot[2][k] * off[2]) for k in range(3)]
    head = [pos[k] - eye[k] for k in range(3)]
    inv_len = 1.0 / jnp.sqrt(head[0] * head[0] + head[1] * head[1] + head[2] * head[2])
    basis = harmonics(head[0] * inv_len, head[1] * inv_len, head[2] * inv_len)
    colours = []
    for k in range(3):
        total = 0.5 + 0.28209479177387814 * raw(11 + k)
        for j in range(1, 16):
            total = total + basis[j] * raw(11 + 3 * j + k)
        colours.append(jnp.maximum(total, 0.0))
    log_o = jnp.maximum(-LOG2E * jnp.log1p(jnp.exp(-raw(10))), NEG)
    log_o = jnp.where(seen > 0, log_o, NEG)
    return [
        sx,
        sy,
        (-0.5 * LOG2E) * (cov_c * inv_det),
        LOG2E * (cov_b * inv_det),
        (-0.5 * LOG2E) * (cov_a * inv_det),
        log_o,
    ] + colours


def cells_in_turn(my_c, own, body):
    order = (4, 3, 5, 2, 6, 1, 7, 0)

    def eight(i, carry):
        place = (my_c + i + 1) & 15
        for step in order:
            body(((my_c + 16 * step) & (CELLS - 16)) + place)
        return carry

    lax.fori_loop(0, 15, eight, 0)
    place = my_c & 15
    for step in order[:7]:
        body(((my_c + 16 * step) & (CELLS - 16)) + place)
    if not own:
        body(my_c)


def kernel(
    params,
    visible,
    cam,
    tile_ids,
    tile_blocks,
    target,
    image_out,
    loss_out,
    par_s,
    vis_s,
    tid_i,
    blk_i,
    list_s,
    pick,
    req,
    rreq,
    view_s,
    feat,
    grid_f,
    px_s,
    sbuf0,
    sbuf1,
    rbuf0,
    rbuf1,
    s2buf0,
    s2buf1,
    r2buf0,
    r2buf1,
    tpad,
    ipad,
    edge_out,
    edge_in,
    vert,
    blur_t,
    blur_i,
    load_sem,
    small_sem,
    req_send,
    req_recv,
    halo_send,
    halo_recv,
    one_send,
    one_recv,
    two_send,
    two_recv,
):
    my_c = lax.axis_index("cell")
    my_v = lax.axis_index("view")
    me_slot = my_v * CELLS + my_c

    barrier = pltpu.get_barrier_semaphore()

    small = [
        pltpu.make_async_copy(tile_ids, tid_i, small_sem.at[0]),
        pltpu.make_async_copy(tile_blocks, blk_i, small_sem.at[1]),
        pltpu.make_async_copy(target, tpad.at[:, pl.ds(8, 16), pl.ds(0, 1920)], small_sem.at[2]),
    ]
    for copy in small:
        copy.start()

    def greet(cell):
        pl.semaphore_signal(barrier, inc=1, device_id=(cell, my_v), device_id_type=MESH)
        pl.semaphore_signal(barrier, inc=1, device_id=(cell, 1 - my_v), device_id_type=MESH)

    pl.semaphore_signal(barrier, inc=1, device_id=(my_c, 1 - my_v), device_id_type=MESH)
    cells_in_turn(my_c, True, greet)

    tpad[:, :, 1920:2048] = jnp.zeros((3, 32, 128), F32)
    ipad[:, :, 1920:2048] = jnp.zeros((3, 32, 128), F32)
    par_s[:, NB:NBP, :] = jnp.zeros((59, NBP - NB, 128), F32)
    vis_s[:, NB:NBP, :] = jnp.zeros((4, NBP - NB, 128), jnp.int32)

    def load(b, carry):
        lanes = pl.ds(pl.multiple_of(b * 128, 128), 128)
        pltpu.make_async_copy(params.at[:, lanes], par_s.at[:, b, :], load_sem.at[0]).start()
        pltpu.make_async_copy(visible.at[:, lanes], vis_s.at[:, b, :], load_sem.at[1]).start()
        return carry

    lax.fori_loop(0, NB, load, 0)

    list_s[...] = jnp.full((8, 128), -1.0, F32)
    small[0].wait()
    small[1].wait()
    list_s[0:1, 0:TILES] = tid_i[...].astype(F32)
    list_s[1:3, 0:TILES] = blk_i[...].astype(F32)
    lists = jnp.transpose(list_s[...])[0:TILES].astype(jnp.int32)
    tid = lists[:, 0:1]
    stripe = quotient(tid, TILES)
    column = tid - TILES * stripe
    lane2 = iota((TILES, 256), 1)
    hits = []
    local = []
    for entry in range(2):
        block = lists[:, 1 + entry : 2 + entry]
        owner = quotient(jnp.maximum(block, 0), NB)
        cell = owner // 2
        slot = (owner - 2 * cell) * CELLS + cell
        slot = jnp.where(block >= 0, slot, -1)
        hits.append((slot == lane2).astype(F32))
        local.append((block - NB * owner + 1).astype(F32))
    by_stripe = (stripe == iota((TILES, 128), 1)).astype(F32)
    lb_row = jnp.sum(hits[0] * local[0] + hits[1] * local[1], axis=0, keepdims=True) - 1.0
    tl_row = jnp.sum((hits[0] + hits[1]) * tid.astype(F32), axis=0, keepdims=True)
    col_row = jnp.sum(by_stripe * (column + 1).astype(F32), axis=0, keepdims=True) - 1.0
    sub = iota((128, 128), 0)
    for part in range(2):
        lanes = slice(128 * part, 128 * (part + 1))
        text = jnp.where(
            sub < 32, lb_row[:, lanes], jnp.where(sub < 64, tl_row[:, lanes], col_row)
        )
        req[lanes, 0, :] = jnp.transpose(text).astype(jnp.int32)
    stripe_hot = by_stripe.astype(BF16)
    for entry in range(2):
        rows = slice(128 * entry, 128 * (entry + 1))
        pick[rows, :] = dot00(stripe_hot, hits[entry].astype(BF16)).astype(BF16)
    small[2].wait()

    pl.semaphore_wait(barrier, 2 * CELLS - 1)

    def exchange(src, dst, rows, send, recv, view, first):
        def go(cell):
                pltpu.make_async_remote_copy(
                src_ref=src.at[view * CELLS + cell, pl.ds(0, rows)],
                dst_ref=dst.at[me_slot, pl.ds(0, rows)],
                send_sem=send,
                recv_sem=recv,
                device_id=(cell, view),
                device_id_type=MESH,
            ).start()

        cells_in_turn(my_c, first == 1, go)

    def settle(ref, count, rows, sem):
        part = ref.at[pl.ds(0, count), pl.ds(0, rows)]
        pltpu.make_async_copy(part, part, sem).wait()

    exchange(req, rreq, 1, req_send, req_recv, my_v, 1)
    exchange(req, rreq, 1, req_send, req_recv, 1 - my_v, 0)

    above = lax.rem(my_c + CELLS - 1, CELLS)
    below = lax.rem(my_c + 1, CELLS)

    def halo(buf, number, way):
        if way:
            edge_out[number, :, 0:5, :] = buf[:, 19:24, 0:1920]
            src, dst = edge_out.at[number, :, pl.ds(0, 5), :], edge_in.at[number, :, pl.ds(0, 5), :]
        else:
            lanes = pl.ds(0, 1920)
            src, dst = buf.at[:, pl.ds(8, 5), lanes], buf.at[:, pl.ds(24, 5), lanes]
        copy = pltpu.make_async_remote_copy(
            src_ref=src,
            dst_ref=dst,
            send_sem=halo_send.at[2 * number + way],
            recv_sem=halo_recv.at[2 * number + way],
            device_id=(below if way else above, my_v),
            device_id_type=MESH,
        )
        copy.start()
        return copy

    target_halo = [halo(tpad, 0, way) for way in range(2)]
    rreq[me_slot] = req[me_slot]
    settle(rreq, 255, 1, req_recv)

    asked = rreq[:, 0, :].astype(F32)
    turned = jnp.concatenate(
        [jnp.transpose(asked[0:128]), jnp.transpose(asked[128:256])], axis=1
    )
    want = turned[0:1, :].astype(jnp.int32)
    tile = turned[32:33, :].astype(jnp.int32)
    cols_in = jnp.where(my_v == 0, turned[64:65, 0:128], turned[64:65, 128:256]).astype(jnp.int32)
    t_stripe = quotient(tile, TILES)
    t_col = tile - TILES * t_stripe
    place = t_stripe - CELLS // 4
    place = jnp.where(place < 0, place + CELLS, place)
    side = (place >= CELLS // 2).astype(jnp.int32)
    anchor_x = (16 * t_col).astype(F32)
    anchor_y = (16 * (place - (CELLS // 2) * side)).astype(F32)
    view_d = (2 * (iota((1, 256), 1) // CELLS) + side).astype(F32)
    hot = (iota((NBP, 256), 0) == want).astype(F32)
    view_s[...] = jnp.broadcast_to(jnp.sum(hot * view_d, axis=1, keepdims=True), (NBP, 128))
    hot16 = hot.astype(BF16)

    pltpu.make_async_copy(par_s.at[:, pl.ds(0, NB), :], par_s.at[:, pl.ds(0, NB), :], load_sem.at[0]).wait()
    pltpu.make_async_copy(vis_s.at[:, pl.ds(0, NB), :], vis_s.at[:, pl.ds(0, NB), :], load_sem.at[1]).wait()

    def project(i, carry):
        rows = pl.ds(pl.multiple_of(8 * i, 8), 8)
        view = view_s[rows, :]
        seen = jnp.where(
            view < 1.5,
            jnp.where(view < 0.5, vis_s[0, rows, :], vis_s[1, rows, :]),
            jnp.where(view < 2.5, vis_s[2, rows, :], vis_s[3, rows, :]),
        )
        found = project_chunk(lambda f: par_s[f, rows, :], seen, cam, view)
        inside = iota((8, 128), 0) + 8 * i < NB
        for f in range(9):
            feat[f, rows, :] = jnp.where(inside, found[f], 0.0)
        return carry

    lax.fori_loop(0, NBP // 8, project, 0)

    live = want >= 0
    for f in range(9):
        high, mid, low = pieces(feat[f])
        got = (dot00(low, hot16) + dot00(mid, hot16)) + dot00(high, hot16)
        if f == 0:
            got = got - anchor_x
        if f == 1:
            got = got - anchor_y
        if f == 5:
            got = jnp.where(live, got, NEG)
        grid_f[0, f] = got[:, 0:128]
        grid_f[1, f] = got[:, 128:256]

    sub8 = iota((8, 128), 0).astype(F32)

    def render(view, part, sbuf):
        for quarter in (2 * part, 2 * part + 1):

            def blend(g, state):
                state = list(state)
                row = [
                    jnp.broadcast_to(grid_f[view, f, pl.ds(g, 1), :], (8, 128)) for f in range(9)
                ]
                dx = [sub8 - row[0], (sub8 + 8.0) - row[0]]
                lead = [row[2] * d * d + row[5] for d in dx]
                cross = [row[3] * d for d in dx]
                dy = 4.0 * quarter - row[1]
                bend = row[4] * dy
                slope = (bend + bend) + row[4]
                curve = row[4] + row[4]
                power = [lead[half] + dy * (cross[half] + bend) for half in range(2)]
                rise = [cross[half] + slope for half in range(2)]
                for line in range(4):
                    for half in range(2):
                        at = 4 * (2 * line + half)
                        alpha = jnp.exp2(power[half])
                        if line < 3:
                            power[half] = power[half] + rise[half]
                        if line < 2:
                            rise[half] = rise[half] + curve
                        weight = alpha * state[at + 3]
                        state[at] = state[at] + weight * row[6]
                        state[at + 1] = state[at + 1] + weight * row[7]
                        state[at + 2] = state[at + 2] + weight * row[8]
                        state[at + 3] = state[at + 3] - weight
                return tuple(state)

            zero = jnp.zeros((8, 128), F32)
            one = jnp.ones((8, 128), F32)
            state = lax.fori_loop(0, 128, blend, (zero, zero, zero, one) * 8, unroll=4)
            for at in range(8):
                start = 64 * (quarter % 2) + 8 * at
                for k in range(4):
                    px_s[k, start : start + 8, :] = state[4 * at + k]
        rows = pl.ds(pl.multiple_of(view * CELLS, CELLS), CELLS)
        for k in range(4):
            sbuf[rows, k, :] = jnp.transpose(px_s[k])

    sent = [sbuf0, sbuf1]
    got = [rbuf0, rbuf1]
    for part in range(2):
        render(my_v, part, sent[part])
        exchange(sent[part], got[part], 4, one_send.at[part], one_recv.at[part], my_v, 1)
        got[part][me_slot] = sent[part][me_slot]
        render(1 - my_v, part, sent[part])
        exchange(sent[part], got[part], 4, one_send.at[part], one_recv.at[part], 1 - my_v, 0)

    taps = [0.0] * 6
    total = sum(2.718281828459045 ** (-(k * k) / 4.5) for k in range(-5, 6))
    for k in range(6):
        taps[k] = 2.718281828459045 ** (-(k * k) / 4.5) / total

    spot = lax.rem(my_c + CELLS - CELLS // 4, CELLS // 2)
    keep_top = jnp.where(spot != 0, 1.0, 0.0)
    keep_bottom = jnp.where(spot != CELLS // 2 - 1, 1.0, 0.0)

    def down_columns(terms):
        totals = [taps[0] * v for v in terms(0)]
        for k in range(1, 6):
            lower, upper = terms(-k), terms(k)
            totals = [t + taps[k] * (a + b) for t, a, b in zip(totals, lower, upper)]
        return totals

    def spread(x):
        acc = taps[0] * x
        for k in range(1, 6):
            acc = acc + taps[k] * (pltpu.roll(x, k, 1) + pltpu.roll(x, 2048 - k, 1))
        return acc[:, 0:1920]

    def along_rows(i, carry):
        rows = pl.ds(pl.multiple_of(8 * (i % 2), 8), 8)
        blur_t[i // 2, rows, :] = spread(vert[i // 2, rows, :])
        return carry

    def image_rows(group):
        rows = slice(8 * group, 8 * group + 8)

        def go(ch, carry):
            x = ipad[ch, rows, :]
            for n, plane in enumerate((x, x * x, x * tpad[ch, rows, :])):
                blur_i[3 * n + ch, rows, :] = spread(plane)
            return carry

        lax.fori_loop(0, 3, go, 0, unroll=3)

    for copy in target_halo:
        copy.wait()
    tpad[:, 3:8, 0:1920] = edge_in[0, :, 0:5, :] * keep_top
    tpad[:, 24:29, 0:1920] = tpad[:, 24:29, 0:1920] * keep_bottom
    vert[:, :, 1920:2048] = jnp.zeros((6, 16, 128), F32)

    def target_columns(j, carry):
        lanes = pl.ds(pl.multiple_of(128 * j, 128), 128)
        for ch in range(3):

            def terms(k):
                t = tpad[ch, 8 + k : 24 + k, lanes]
                return [t, t * t]

            found = down_columns(terms)
            vert[ch, :, lanes] = found[0]
            vert[3 + ch, :, lanes] = found[1]
        return carry

    lax.fori_loop(0, 15, target_columns, 0)
    lax.fori_loop(0, 12, along_rows, 0, unroll=6)

    settle(req, 255, 1, req_send)
    sent2 = [s2buf0, s2buf1]
    got2 = [r2buf0, r2buf1]

    for part in range(2):
        tiles, out, arrived = got[part], sent2[part], got2[part]
        settle(tiles, 255, 4, one_recv.at[part])

        hot = pick[...]
        pairs = []
        for k in (0, 2):
            parts = pieces(jnp.concatenate([tiles[:, k, :], tiles[:, k + 1, :]], axis=1))
            pairs.append((dot10(hot, parts[2]) + dot10(hot, parts[1])) + dot10(hot, parts[0]))
        clear = pairs[1][0:128, 128:256]
        for k in range(3):
            pair, lanes = pairs[k // 2], slice(128 * (k % 2), 128 * (k % 2) + 128)
            out[:, k, :] = pair[0:128, lanes] + clear * pair[128:256, lanes]

        def send_tile(cell):
                pltpu.make_async_remote_copy(
                src_ref=out.at[cell, pl.ds(0, 3)],
                dst_ref=arrived.at[my_c, pl.ds(0, 3)],
                send_sem=two_send.at[part],
                recv_sem=two_recv.at[part],
                device_id=(cell, my_v),
                device_id_type=MESH,
            ).start()

        cells_in_turn(my_c, True, send_tile)
        arrived[my_c] = out[my_c]
    settle(sbuf0, 255, 4, one_send.at[0])
    settle(sbuf1, 255, 4, one_send.at[1])

    hot_col = (iota((TILES, 128), 0) == cols_in).astype(BF16)
    sub_b = iota((15, 8, 128), 1)
    lane_b = iota((15, 8, 128), 2) // 16

    image_halo = []
    for part in range(2):
        settle(got2[part], 127, 3, two_recv.at[part])
        for ch in range(3):
            parts = pieces(got2[part][:, ch, :])
            found = (dot10(hot_col, parts[2]) + dot10(hot_col, parts[1])) + dot10(hot_col, parts[0])
            cube = found.reshape(15, 8, 128)
            for bit in (1, 2, 4):
                sub_bit = (sub_b & bit) != 0
                lane_bit = (lane_b & bit) != 0
                from_up = pltpu.roll(pltpu.roll(cube, bit, 1), 128 - 16 * bit, 2)
                from_down = pltpu.roll(pltpu.roll(cube, 8 - bit, 1), 16 * bit, 2)
                cube = jnp.where(sub_bit == lane_bit, cube, jnp.where(sub_bit, from_up, from_down))
            for j in range(15):
                ipad[ch, 8 + 8 * part : 16 + 8 * part, 128 * j : 128 * (j + 1)] = cube[j]
        image_halo.append(halo(ipad, 1, part))
        if part == 0:
            image_rows(1)

    inner = ipad.at[:, pl.ds(8, 16), pl.ds(0, 1920)]
    image_copy = pltpu.make_async_copy(inner, image_out, small_sem.at[3])
    image_copy.start()
    image_rows(2)
    image_halo[0].wait()
    ipad[:, 24:29, 0:1920] = ipad[:, 24:29, 0:1920] * keep_bottom
    image_rows(3)
    for part in range(2):
        settle(sent2[part], 127, 3, two_send.at[part])
    image_halo[1].wait()
    ipad[:, 3:8, 0:1920] = edge_in[1, :, 0:5, :] * keep_top
    image_rows(0)

    def finish(j, carry):
        lanes = pl.ds(pl.multiple_of(128 * j, 128), 128)
        apart = jnp.zeros((16, 128), F32)
        alike = jnp.zeros((16, 128), F32)
        for ch in range(3):

            def terms(k):
                return [blur_i[3 * n + ch, 8 + k : 24 + k, lanes] for n in range(3)]

            mx, sxx, sxy = down_columns(terms)
            my, syy = blur_t[ch, :, lanes], blur_t[3 + ch, :, lanes]
            mxx, myy, mxy = mx * mx, my * my, mx * my
            above_line = (2.0 * mxy + 0.0001) * (2.0 * (sxy - mxy) + 0.0009)
            below_line = (mxx + myy + 0.0001) * ((sxx - mxx) + (syy - myy) + 0.0009)
            alike = alike + above_line / below_line
            apart = apart + jnp.abs(ipad[ch, 8:24, lanes] - tpad[ch, 8:24, lanes])
        loss_out[:, lanes] = 0.8 * (apart * (1.0 / 3.0)) + 0.2 * (1.0 - alike * (1.0 / 3.0))
        return carry

    lax.fori_loop(0, 15, finish, 0)
    image_copy.wait()


def local(gauss_params, visible, cameras, tile_ids, tile_blocks, target):
    vmem = pl.BlockSpec(memory_space=pltpu.VMEM)
    hbm = pl.BlockSpec(memory_space=pltpu.HBM)
    dma = pltpu.SemaphoreType.DMA
    image, loss = pl.pallas_call(
        kernel,
        out_shape=(
            jax.ShapeDtypeStruct((3, 16, 1920), F32),
            jax.ShapeDtypeStruct((16, 1920), F32),
        ),
        in_specs=[hbm, hbm, pl.BlockSpec(memory_space=pltpu.SMEM), hbm, hbm, hbm],
        out_specs=(hbm, vmem),
        scratch_shapes=[
            pltpu.VMEM((59, NBP, 128), F32),
            pltpu.VMEM((4, NBP, 128), jnp.int32),
            pltpu.VMEM((1, TILES), jnp.int32),
            pltpu.VMEM((2, TILES), jnp.int32),
            pltpu.VMEM((8, 128), F32),
            pltpu.VMEM((256, 256), BF16),
            pltpu.VMEM((256, 1, 128), jnp.int32),
            pltpu.VMEM((256, 1, 128), jnp.int32),
            pltpu.VMEM((NBP, 128), F32),
            pltpu.VMEM((9, NBP, 128), F32),
            pltpu.VMEM((2, 9, 128, 128), F32),
            pltpu.VMEM((4, 128, 128), F32),
            pltpu.VMEM((256, 4, 128), F32),
            pltpu.VMEM((256, 4, 128), F32),
            pltpu.VMEM((256, 4, 128), F32),
            pltpu.VMEM((256, 4, 128), F32),
            pltpu.VMEM((128, 4, 128), F32),
            pltpu.VMEM((128, 4, 128), F32),
            pltpu.VMEM((128, 4, 128), F32),
            pltpu.VMEM((128, 4, 128), F32),
            pltpu.VMEM((3, 32, 2048), F32),
            pltpu.VMEM((3, 32, 2048), F32),
            pltpu.VMEM((2, 3, 8, 1920), F32),
            pltpu.VMEM((2, 3, 8, 1920), F32),
            pltpu.VMEM((6, 16, 2048), F32),
            pltpu.VMEM((6, 16, 1920), F32),
            pltpu.VMEM((9, 32, 1920), F32),
            dma((2,)),
            dma((4,)),
            dma,
            dma,
            dma((4,)),
            dma((4,)),
            dma((2,)),
            dma((2,)),
            dma((2,)),
            dma((2,)),
        ],
        compiler_params=pltpu.CompilerParams(
            collective_id=0, has_side_effects=True, vmem_limit_bytes=60 << 20
        ),
    )(gauss_params, visible, cameras, tile_ids[0], tile_blocks[0, 0].T, target[0])
    return (image[None], loss[None])


def solution(mesh):
    return jax.shard_map(
        local,
        mesh=mesh,
        in_specs=(
            P(None, ("cell", "view")),
            P(None, ("cell", "view")),
            P(),
            P("cell", "view", None),
            P("cell", "view", None, None),
            P("view", None, "cell", None),
        ),
        out_specs=(P("view", None, "cell", None), P("view", "cell", None)),
        check_vma=False,
    )
```
